256 devices in a mesh: dom: 64 (over z, y, core), local: 4 (over x).
Axes of the slice: x: 4, y: 4, z: 8, core: 2. Of those that a mesh axis runs over, the one named last changes fastest.
Arguments:
- features: bfloat16 [1048576, 256], P(('dom', 'local')), may hold values from -6 to 6
- w_self: bfloat16 [256, 128], replicated, may hold values from -0.375 to 0.375
- w_neigh: bfloat16 [256, 128], replicated, may hold values from -0.375 to 0.375
- bias_vector: float32 [128], replicated, may hold values from -3 to 3
- adjacency: bfloat16 [49152, 128, 128], P(('dom', 'local')), may hold values from 0 to 1, as said below
- tile_at: int32 [49152, 2], P(('dom', 'local')), may hold values from 0 to 47, as said below
- clone_root: int32 [256, 256, 8], P(('dom', 'local')), may hold values from 0 to 4095, as said below
- clone_count: int32 [256, 256], P(('dom', 'local')), may hold values from 1 to 8, as said below
- degrees: int32 [1048576], P(('dom', 'local')), may hold values from 16 to 63
- cotangent: bfloat16 [1048576, 128], P(('dom', 'local')), may hold values from -6 to 6
Outputs:
- activation: bfloat16 [1048576, 128], P(('dom', 'local'))
- grad_features: bfloat16 [1048576, 256], P(('dom', 'local'))
- grad_self: float32 [256, 128], replicated
- grad_neigh: float32 [256, 128], replicated
The draws below stay inside these ranges and needn't reach their ends.
Inputs may be any that keep to these rules, and one draw needn't show every extreme that they name: `adjacency`: entries are 0 or 1. `tile_at`: column 0 is a tile's destination block among the device's slot rows, column 1 its source block among the device's own nodes; every destination block of a device is named by at least one of its tiles. `clone_root`: the live entries of one bucket (e, d) are distinct. Every device e has some sender d with clone_count[e, d] = 8.
All inputs are finite; a program needn't handle non-finite values.
Results may differ from the reference program's by a relative error of at most 0.0052.
Values may be sent and summed in bfloat16 or wider, within the bound.
A program may use at most 128 MiB of HBM per device.

```python
import jax
import jax.numpy as jnp
from jax import lax

F_IN = 256
F_OUT = 128
BLOCK = 128
ROOTS_DEV = 4096
CLONES_DEV = 2048
TILES_DEV = 192
DEVS = 256
CAPACITY = 8
NODES = 1048576


def draw_adjacency(key, part):
    key = jax.random.fold_in(key, 1)
    uniform_vals = jax.random.uniform(key, (DEVS * TILES_DEV, BLOCK, BLOCK), jnp.float32)
    return (uniform_vals < 0.0625).astype(jnp.bfloat16)


def draw_tile_at(key, part):
    key = jax.random.fold_in(key, 2)
    key_extra, key_order, key_source = jax.random.split(key, 3)
    dest_count = (ROOTS_DEV + CLONES_DEV) // BLOCK
    source_count = ROOTS_DEV // BLOCK
    cover = jnp.broadcast_to(jnp.arange(dest_count, dtype=jnp.int32)[None, :], (DEVS, dest_count))
    extra = jax.random.randint(key_extra, (DEVS, TILES_DEV - dest_count), 0, dest_count, dtype=jnp.int32)
    dest = jnp.concatenate([cover, extra], axis=1)
    scores = jax.random.randint(key_order, (DEVS, TILES_DEV), 0, 1 << 20, dtype=jnp.int32) * TILES_DEV + jnp.arange(TILES_DEV, dtype=jnp.int32)[None, :]
    order = jnp.argsort(scores, axis=1, stable=True)
    dest = jnp.take_along_axis(dest, order, axis=1)
    source = jax.random.randint(key_source, (DEVS, TILES_DEV), 0, source_count, dtype=jnp.int32)
    return jnp.stack([dest, source], axis=-1).reshape(DEVS * TILES_DEV, 2).astype(jnp.int32)


def draw_clone_root(key, part):
    key = jax.random.fold_in(key, 3)
    key_start, key_step, key_order = jax.random.split(key, 3)
    start = jax.random.randint(key_start, (DEVS, DEVS, 1), 0, ROOTS_DEV, dtype=jnp.int32)
    steps = jax.random.randint(key_step, (DEVS, DEVS, CAPACITY), 1, ROOTS_DEV // CAPACITY + 1, dtype=jnp.int32)
    steps = jnp.where(jnp.arange(CAPACITY, dtype=jnp.int32)[None, None, :] == 0, 0, steps)
    values = (start + jnp.cumsum(steps, axis=-1)) % ROOTS_DEV
    scores = jax.random.randint(key_order, (DEVS, DEVS, CAPACITY), 0, 1 << 16, dtype=jnp.int32) * CAPACITY + jnp.arange(CAPACITY, dtype=jnp.int32)[None, None, :]
    order = jnp.argsort(scores, axis=-1, stable=True)
    return jnp.take_along_axis(values, order, axis=-1).astype(jnp.int32)


def draw_clone_count(key, part):
    key = jax.random.fold_in(key, 4)
    key_first, key_second, key_full = jax.random.split(key, 3)
    first = jax.random.randint(key_first, (DEVS, DEVS), 1, CAPACITY + 1, dtype=jnp.int32)
    second = jax.random.randint(key_second, (DEVS, DEVS), 1, CAPACITY + 1, dtype=jnp.int32)
    counts = jnp.maximum(first, second)
    full_sender = jax.random.randint(key_full, (DEVS,), 0, DEVS, dtype=jnp.int32)
    is_full = jnp.arange(DEVS, dtype=jnp.int32)[None, :] == full_sender[:, None]
    return jnp.where(is_full, CAPACITY, counts).astype(jnp.int32)


def set_ends(array, rng, smallest, high):
    dims = array.shape
    index_at = [jax.random.randint(jax.random.fold_in(rng, axis), (), 0, dims[axis]) for axis in range(len(dims))]
    array = array.at[tuple(index_at)].set(smallest)
    longest = dims.index(max(dims))
    index_at[longest] = (index_at[longest] + 1) % dims[longest]
    return array.at[tuple(index_at)].set(high)


def steps_of(own_key, extent, cuts, least, largest):
    def one(position, shards_of):
        draws = jax.random.uniform(jax.random.fold_in(jax.random.fold_in(own_key, 6), position), (shards_of,), jnp.float32, least / len(cuts), largest / len(cuts))
        return jnp.repeat(jnp.exp(draws), extent[position] // shards_of).reshape((-1,) + (1,) * (len(extent) - position - 1))

    loudness = one(*cuts[0])
    for cut in cuts[1:]:
        loudness = loudness * one(*cut)
    return loudness


def bell_draw(own_key, extent, deviation, bound, cuts=(), kind=jnp.bfloat16):
    array = jax.random.normal(own_key, extent, jnp.float32) * deviation
    if len(cuts) > 0:
        array = steps_of(own_key, extent, cuts, -0.22, 0.18) * array
    return jnp.clip(array, min=-bound, max=bound).astype(kind)


def setup_inputs(seed: int = 0) -> dict:
    key_of = jax.random.split(jax.random.key(seed), 11)
    return {
        "features": bell_draw(key_of[0], (NODES, F_IN), 1.0, 6.0, ((0, 256),)),
        "w_self": bell_draw(key_of[1], (F_IN, F_OUT), F_IN ** -0.5, 0.375),
        "w_neigh": bell_draw(key_of[2], (F_IN, F_OUT), F_IN ** -0.5, 0.375),
        "bias_vector": bell_draw(key_of[3], (F_OUT,), 0.5, 3.0, (), jnp.float32),
        "adjacency": draw_adjacency(jax.random.fold_in(key_of[10], 71), 0),
        "tile_at": draw_tile_at(jax.random.fold_in(key_of[10], 71), 0),
        "clone_root": draw_clone_root(jax.random.fold_in(key_of[10], 71), 0),
        "clone_count": draw_clone_count(jax.random.fold_in(key_of[10], 71), 0),
        "degrees": set_ends(jax.random.randint(key_of[8], (NODES,), 512 * TILES_DEV // (ROOTS_DEV + CLONES_DEV), 2048 * TILES_DEV // (ROOTS_DEV + CLONES_DEV)), jax.random.fold_in(key_of[8], 1), 512 * TILES_DEV // (ROOTS_DEV + CLONES_DEV), (2048 * TILES_DEV // (ROOTS_DEV + CLONES_DEV)) - 1).astype(jnp.int32),
        "cotangent": bell_draw(key_of[9], (NODES, F_OUT), 1.0, 6.0, ((0, 256),)),
    }


def aggregate(pack):
    adjacency_dev, tile_pos, projected_dev = pack
    source_rows = projected_dev.astype(jnp.float32).reshape(ROOTS_DEV // BLOCK, BLOCK, F_OUT)[tile_pos[:, 1]]
    products = jnp.einsum("tij,tjf->tif", adjacency_dev.astype(jnp.float32), source_rows, precision=lax.Precision.HIGHEST)
    dest_count = (ROOTS_DEV + CLONES_DEV) // BLOCK
    onehot = (tile_pos[:, 0][None, :] == jnp.arange(dest_count, dtype=jnp.int32)[:, None]).astype(jnp.float32)
    summed = jnp.einsum("bt,tif->bif", onehot, products, precision=lax.Precision.HIGHEST)
    return summed.reshape(ROOTS_DEV + CLONES_DEV, F_OUT)


def spread(pack):
    adjacency_dev, tile_pos, slot_dev = pack
    dest_rows = slot_dev.astype(jnp.float32).reshape((ROOTS_DEV + CLONES_DEV) // BLOCK, BLOCK, F_OUT)[tile_pos[:, 0]]
    products = jnp.einsum("tij,tif->tjf", adjacency_dev.astype(jnp.float32), dest_rows, precision=lax.Precision.HIGHEST)
    onehot = (tile_pos[:, 1][None, :] == jnp.arange(ROOTS_DEV // BLOCK, dtype=jnp.int32)[:, None]).astype(jnp.float32)
    summed = jnp.einsum("st,tjf->sjf", onehot, products, precision=lax.Precision.HIGHEST)
    return summed.reshape(ROOTS_DEV, F_OUT)


def collect(pack):
    own_rows, clone_rows, targets, is_live = pack
    values = jnp.where(is_live[:, :, None], clone_rows, jnp.zeros((), clone_rows.dtype)).reshape(DEVS * CAPACITY, F_OUT)
    return own_rows.at[targets.reshape(DEVS * CAPACITY)].add(values)


def hand_back(pack):
    grad_rows, targets, is_live = pack
    picked = grad_rows[targets.reshape(DEVS * CAPACITY)].reshape(DEVS, CAPACITY, F_OUT)
    return jnp.where(is_live[:, :, None], picked, jnp.zeros((), picked.dtype))


def reference(features, w_self, w_neigh, bias_vector, adjacency, tile_at, clone_root, clone_count, degrees, cotangent):
    tiles_all = adjacency.reshape(DEVS, TILES_DEV, BLOCK, BLOCK)
    tile_pos = tile_at.reshape(DEVS, TILES_DEV, 2)
    projected = jnp.dot(features, w_neigh, preferred_element_type=jnp.float32).astype(jnp.bfloat16)
    partial_value = lax.map(aggregate, (tiles_all, tile_pos, projected.reshape(DEVS, ROOTS_DEV, F_OUT)))
    clone_part = partial_value[:, ROOTS_DEV:].astype(jnp.bfloat16)
    clone_part = lax.optimization_barrier(clone_part).astype(jnp.float32)
    clone_rows = clone_part.reshape(DEVS, DEVS, CAPACITY, F_OUT).transpose(1, 0, 2, 3)
    is_live = jnp.arange(CAPACITY, dtype=jnp.int32)[None, None, :] < clone_count[:, :, None]
    total = lax.map(collect, (partial_value[:, :ROOTS_DEV], clone_rows, clone_root, is_live)).reshape(NODES, F_OUT)
    degree_f = degrees.astype(jnp.float32)[:, None]
    preact = jnp.dot(features, w_self, preferred_element_type=jnp.float32) + total / degree_f + bias_vector[None, :]
    sigmoid_val = jax.nn.sigmoid(preact)
    activation = (preact * sigmoid_val).astype(jnp.bfloat16)
    grad_full = cotangent.astype(jnp.float32) * sigmoid_val * (1.0 + preact * (1.0 - sigmoid_val))
    grad_pre = grad_full.astype(jnp.bfloat16)
    grad_mean = (grad_full / degree_f).astype(jnp.bfloat16)
    grad_dev = grad_mean.reshape(DEVS, ROOTS_DEV, F_OUT)
    sent = lax.map(hand_back, (grad_dev, clone_root, is_live))
    clone_grad = sent.transpose(1, 0, 2, 3).reshape(DEVS, CLONES_DEV, F_OUT)
    slot_grad = jnp.concatenate([grad_dev, clone_grad], axis=1)
    grad_proj = lax.map(spread, (tiles_all, tile_pos, slot_grad)).astype(jnp.bfloat16).reshape(NODES, F_OUT)
    grad_features = (jnp.dot(grad_pre, w_self.T, preferred_element_type=jnp.float32)
                     + jnp.dot(grad_proj, w_neigh.T, preferred_element_type=jnp.float32)).astype(jnp.bfloat16)
    scale_factor = float(NODES) ** -0.5
    grad_self = jnp.dot(features.T, grad_pre, preferred_element_type=jnp.float32) * scale_factor
    grad_neigh = jnp.dot(features.T, grad_proj, preferred_element_type=jnp.float32) * scale_factor
    return (activation, grad_features, grad_self, grad_neigh)
```

```python
import functools

import jax
import jax.numpy as jnp
from jax import lax
from jax.experimental import pallas as pl
from jax.experimental.pallas import tpu as pltpu
from jax.sharding import PartitionSpec as P

MESH = pl.DeviceIdType.MESH
F32 = jnp.float32
BF16 = jnp.bfloat16

NZ, NY, NX = 8, 4, 4
NXY = NY * NX
CAP = 8
BLOCK = 128
TILES = 192
OWN_BLOCKS = 32
CLONE_BLOCKS = 16
DEST_BLOCKS = OWN_BLOCKS + CLONE_BLOCKS
ROOTS = OWN_BLOCKS * BLOCK
MOST_OWN = TILES - CLONE_BLOCKS
MOST_CLONE = TILES - OWN_BLOCKS
PLANE = NXY * 2 * CAP
LOADS = 4

AT_FWD = 0
AT_BWD = AT_FWD + TILES
AT_LAST_FWD = AT_BWD + TILES
AT_LAST_BWD = AT_LAST_FWD + DEST_BLOCKS
TABLE = AT_LAST_BWD + 2 * OWN_BLOCKS


def step_offset(i):
    return 4 + (i // 2) * (1 - i % 2) - ((i + 1) // 2) * (i % 2)


def main_kernel(
    table, slot_s, features_h, weights, bias, adjacency_h, slot_v, degrees, cotangent,
    w_self, w_neigh,
    act_out, gfeat_out, gself_out, gneigh_out,
    feat, adj, proj, own, scan, scan_b, total, gmean, gpre, slots_t, gproj_t, rows_f,
    keep1, pass1, mate1, send1, mid1, land1,
    keep2, pass2, mate2, send2, mid2, land2,
    halves, mate_r, sum_r, z_r, sum_z, xy_r, done,
    load_sems, mate_send, mate_recv, xy_send, xy_recv, z_send, z_recv, own_sems,
    red_send, red_recv,
):
    dom = lax.axis_index("dom")
    x = lax.axis_index("local")
    core = dom % 2
    zy = dom // 2
    z = zy // NY
    y = zy % NY
    xy = y * NX + x
    mate = (dom + 1 - 2 * core, x)

    def xy_peer(k):
        py = (y + k // NX) % NY
        px = (x + k % NX) % NX
        return (z * NY + py) * 2 + core, px, py * NX + px

    def z_peer(dz):
        pz = (z + dz) % NZ
        return ((pz * NY + y) * 2 + core, x), pz

    barrier = pltpu.get_barrier_semaphore()
    pl.semaphore_signal(barrier, inc=1, device_id=mate, device_id_type=MESH)
    for k in range(1, NXY):
        pdom, px, _ = xy_peer(k)
        pl.semaphore_signal(barrier, inc=1, device_id=(pdom, px), device_id_type=MESH)
    for dz in range(1, NZ):
        pl.semaphore_signal(barrier, inc=1, device_id=z_peer(dz)[0], device_id_type=MESH)

    load_feat = pltpu.make_async_copy(features_h, feat, load_sems.at[LOADS])
    load_feat.start()
    share = TILES // LOADS
    load_adj = [
        pltpu.make_async_copy(
            adjacency_h.at[pl.ds(k * share, share)], adj.at[pl.ds(k * share, share)], load_sems.at[k]
        )
        for k in range(LOADS)
    ]
    for copy in load_adj:
        copy.start()

    load_feat.wait()
    rows = 512

    def project(i, carry):
        both = jnp.dot(feat[pl.ds(i * rows, rows), :], weights[...], preferred_element_type=F32)
        proj[pl.ds(i * (rows // BLOCK), rows // BLOCK)] = both[:, :BLOCK].astype(BF16).reshape(rows // BLOCK, BLOCK, BLOCK)
        own[pl.ds(i * (rows // BLOCK), rows // BLOCK)] = (both[:, BLOCK:] + bias[...]).reshape(rows // BLOCK, BLOCK, BLOCK)
        return carry

    lax.fori_loop(0, ROOTS // rows, project, 0, unroll=2)
    for copy in load_adj:
        copy.wait()

    def forward(i, acc):
        code = table[AT_FWD + i]
        tile = code & 255
        source = (code >> 8) & 255
        going = (code >> 24).astype(F32)
        acc = acc * going + jnp.dot(adj[tile], proj[source], preferred_element_type=F32)
        scan[i] = acc
        return acc

    lax.fori_loop(0, TILES, forward, jnp.zeros((BLOCK, BLOCK), F32), unroll=8)

    pl.semaphore_wait(barrier, 1 + (NXY - 1) + (NZ - 1))

    def start_swap(i, value, keep, away, back, lane):
        first = value[:, 0]
        second = value[:, 1]
        keep[i] = jnp.where(core == 0, first, second).reshape(NXY * CAP, BLOCK).astype(BF16)
        away[i] = jnp.where(core == 0, second, first).reshape(NXY * CAP, BLOCK).astype(BF16)
        swap(i, away, back, lane).start()

    def swap(i, away, back, lane):
        return pltpu.make_async_remote_copy(
            away.at[i], back.at[i], mate_send.at[lane, i], mate_recv.at[lane, i], device_id=mate, device_id_type=MESH
        )

    def start_xy(i, keep, away, back, send, mid, lane):
        swap(i, away, back, lane).wait()
        mine = keep[i].astype(F32).reshape(NXY, CAP, BLOCK)
        theirs = back[i].astype(F32).reshape(NXY, CAP, BLOCK)
        first = jnp.where(core == 0, mine, theirs)
        second = jnp.where(core == 0, theirs, mine)
        send[i] = jnp.concatenate([first, second], axis=1).astype(BF16)

        def go(k, carry):
            pdom, px, pxy = xy_peer(k)
            pltpu.make_async_remote_copy(
                send.at[i, pxy], mid.at[i, xy], xy_send.at[lane, i], xy_recv.at[lane, i],
                device_id=(pdom, px), device_id_type=MESH,
            ).start()
            return carry

        lax.fori_loop(1, NXY, go, 0)
        mid[i, xy] = send[i, xy]

    def wait_bytes(ref, sem):
        pltpu.make_async_copy(ref, ref, sem).wait()

    def z_copy(i, mid, land, lane):
        peer, _ = z_peer(step_offset(i))
        return pltpu.make_async_remote_copy(
            mid.at[i], land.at[z], z_send.at[lane, i], z_recv.at[lane, i], device_id=peer, device_id_type=MESH
        )

    def start_z(i, send, mid, land, lane):
        wait_bytes(mid.at[i, pl.ds(0, NXY - 1)], xy_recv.at[lane, i])
        wait_bytes(send.at[i, pl.ds(0, NXY - 1)], xy_send.at[lane, i])

        @pl.when(i < NZ - 1)
        def _():
            z_copy(i, mid, land, lane).start()

        @pl.when(i == NZ - 1)
        def _():
            pltpu.make_async_copy(mid.at[i], land.at[z], own_sems.at[lane]).start()

    def finish_z(i, mid, land, lane):
        @pl.when(i < NZ - 1)
        def _():
            z_copy(i, mid, land, lane).wait()

        @pl.when(i == NZ - 1)
        def _():
            pltpu.make_async_copy(mid.at[i], land.at[z], own_sems.at[lane]).wait()

        return (z + NZ - step_offset(i)) % NZ

    def send_partial(s, carry):
        @pl.when(s < NZ)
        def _():
            pz = (z + step_offset(s)) % NZ
            first = scan[table[AT_LAST_FWD + OWN_BLOCKS + 2 * pz]]
            second = scan[table[AT_LAST_FWD + OWN_BLOCKS + 2 * pz + 1]]
            value = jnp.concatenate([first, second], axis=0).reshape(NY, 2, NX, CAP, BLOCK)
            value = jnp.concatenate([value[:, 0].reshape(NXY, 1, CAP, BLOCK), value[:, 1].reshape(NXY, 1, CAP, BLOCK)], axis=1)
            start_swap(s, value, keep1, pass1, mate1, 0)

        @pl.when((s >= 1) & (s < NZ + 1))
        def _():
            start_xy(s - 1, keep1, pass1, mate1, send1, mid1, 0)

        @pl.when(s >= 3)
        def _():
            start_z(s - 3, send1, mid1, land1, 0)

        return carry

    lax.fori_loop(0, NZ + 3, send_partial, 0)

    def begin_total(b, carry):
        total[b] = scan[table[AT_LAST_FWD + b]]
        return carry

    lax.fori_loop(0, OWN_BLOCKS, begin_total, 0, unroll=4)

    def receive_plane(s, carry):
        plane = finish_z(s, mid1, land1, 0)
        arrived = land1[plane].reshape(PLANE, BLOCK)
        node = slot_v[pl.ds(plane, 1), :]
        row = lax.broadcasted_iota(jnp.int32, (BLOCK, PLANE), 0)

        def add(b, carry):
            hit = jnp.where(row == node - b * BLOCK, 1.0, 0.0).astype(BF16)
            total[b] += jnp.dot(hit, arrived, preferred_element_type=F32)
            return carry

        lax.fori_loop(0, OWN_BLOCKS, add, 0, unroll=4)
        return carry

    lax.fori_loop(0, NZ, receive_plane, 0)

    def activate(b, carry):
        degree = jnp.broadcast_to(degrees[pl.ds(b, 1), :].astype(F32), (BLOCK, BLOCK)).T
        scale = 1.0 / degree
        preact = own[b] + total[b] * scale
        sig = jax.nn.sigmoid(preact)
        act_out[b] = (preact * sig).astype(BF16)
        full = cotangent[b].astype(F32) * sig * (1.0 + preact * (1.0 - sig))
        gpre[b] = full.astype(BF16)
        mean = full * scale
        gmean[pl.ds(b * BLOCK, BLOCK), :] = mean
        slots_t[b] = mean.T.astype(BF16)
        return carry

    lax.fori_loop(0, OWN_BLOCKS, activate, 0, unroll=2)
    gmean[pl.ds(ROOTS, CAP), :] = jnp.zeros((CAP, BLOCK), F32)
    slots_t[DEST_BLOCKS] = jnp.zeros((BLOCK, BLOCK), BF16)
    scan[TILES] = jnp.zeros((BLOCK, BLOCK), F32)
    scan_b[MOST_CLONE] = jnp.zeros((BLOCK, BLOCK), F32)

    def back_own(i, acc):
        code = table[AT_BWD + i]
        tile = code & 255
        dest = (code >> 8) & 255
        going = (code >> 24).astype(F32)
        acc = acc * going + jnp.dot(slots_t[dest], adj[tile], preferred_element_type=F32)
        scan[i] = acc
        return acc

    per_step = MOST_OWN // NZ

    def send_back(s, acc):
        @pl.when(s < NZ)
        def _():
            pz = (z + step_offset(s)) % NZ

            def pick(q, carry):
                for j in range(CAP):
                    rows_f[pl.ds(q * CAP + j, 1), :] = gmean[pl.ds(slot_s[pz * PLANE + q * CAP + j], 1), :]
                return carry

            lax.fori_loop(0, 2 * NXY, pick, 0, unroll=4)
            start_swap(s, rows_f[...].reshape(NXY, 2, CAP, BLOCK), keep2, pass2, mate2, 1)

        @pl.when((s >= 1) & (s < NZ + 1))
        def _():
            start_xy(s - 1, keep2, pass2, mate2, send2, mid2, 1)

        @pl.when(s >= 3)
        def _():
            start_z(s - 3, send2, mid2, land2, 1)

        return acc

    def send_and_work(s, acc):
        send_back(s, 0)
        return lax.fori_loop(0, per_step, lambda i, a: back_own(s * per_step + i, a), acc, unroll=per_step // 2)

    acc = lax.fori_loop(0, NZ, send_and_work, jnp.zeros((BLOCK, BLOCK), F32))
    lax.fori_loop(NZ, NZ + 3, send_back, 0)

    def transposed_gpre(b, carry):
        at = pl.ds(pl.multiple_of(b * BLOCK, BLOCK), BLOCK)
        gproj_t[:, at] = gpre[b].astype(F32).T.astype(BF16)
        return carry

    lax.fori_loop(0, OWN_BLOCKS, transposed_gpre, 0, unroll=4)
    gself = jnp.dot(gproj_t[...], feat[...], preferred_element_type=F32).T

    def arrived_back(s, carry):
        plane = finish_z(s, mid2, land2, 1)
        value = land2[plane].astype(F32).reshape(NY, NX, 2, CAP, BLOCK)
        value = jnp.concatenate(
            [value[:, :, 0].reshape(NY, 1, NX, CAP, BLOCK), value[:, :, 1].reshape(NY, 1, NX, CAP, BLOCK)], axis=1
        ).reshape(2, BLOCK, BLOCK)
        slots_t[OWN_BLOCKS + 2 * plane] = value[0].T.astype(BF16)
        slots_t[OWN_BLOCKS + 2 * plane + 1] = value[1].T.astype(BF16)
        return carry

    lax.fori_loop(0, NZ, arrived_back, 0)

    def back_clone(i, acc):
        code = table[AT_BWD + OWN_BLOCKS + i]
        tile = code & 255
        dest = (code >> 16) & 255
        going = (code >> 24).astype(F32)
        acc = acc * going + jnp.dot(slots_t[dest], adj[tile], preferred_element_type=F32)
        scan_b[i] = acc
        return acc

    lax.fori_loop(0, MOST_CLONE, back_clone, jnp.zeros((BLOCK, BLOCK), F32), unroll=8)

    def gather_proj(c, carry):
        value = scan[table[AT_LAST_BWD + c]] + scan_b[table[AT_LAST_BWD + OWN_BLOCKS + c]]
        at = pl.ds(pl.multiple_of(c * BLOCK, BLOCK), BLOCK)
        gproj_t[:, at] = value.astype(BF16)
        return carry

    lax.fori_loop(0, OWN_BLOCKS, gather_proj, 0, unroll=4)
    gneigh = jnp.dot(gproj_t[...], feat[...], preferred_element_type=F32).T

    part = BLOCK // NZ
    halves[:, :, 0:part] = gself.reshape(2, NZ, part, BLOCK)
    halves[:, :, part:2 * part] = gneigh.reshape(2, NZ, part, BLOCK)
    copy = pltpu.make_async_remote_copy(
        halves.at[1 - core], mate_r, red_send.at[0], red_recv.at[0], device_id=mate, device_id_type=MESH
    )
    copy.start()
    copy.wait()
    sum_r[...] = halves[core] + mate_r[...]

    def along_z(src, dst, k):
        def go(dz, carry):
            peer, pz = z_peer(dz)
            pltpu.make_async_remote_copy(
                src(pz), dst, red_send.at[k], red_recv.at[k], device_id=peer, device_id_type=MESH
            ).start()
            return carry

        lax.fori_loop(1, NZ, go, 0)

    along_z(lambda pz: sum_r.at[pz], z_r.at[z], 1)
    z_r[z] = sum_r[z]
    wait_bytes(z_r.at[pl.ds(0, NZ - 1)], red_recv.at[1])
    wait_bytes(sum_r.at[pl.ds(0, NZ - 1)], red_send.at[1])
    value = z_r[0]
    for k in range(1, NZ):
        value = value + z_r[k]
    sum_z[...] = value

    def go_xy(k, carry):
        pdom, px, _ = xy_peer(k)
        pltpu.make_async_remote_copy(
            sum_z, xy_r.at[xy], red_send.at[2], red_recv.at[2], device_id=(pdom, px), device_id_type=MESH
        ).start()
        return carry

    lax.fori_loop(1, NXY, go_xy, 0)
    xy_r[xy] = sum_z[...]

    def give_features(c, carry):
        at = pl.ds(pl.multiple_of(c * BLOCK, BLOCK), BLOCK)
        value = lax.dot_general(gpre[c], w_self[...], (((1,), (1,)), ((), ())), preferred_element_type=F32)
        value += lax.dot_general(gproj_t[:, at], w_neigh[...], (((0,), (1,)), ((), ())), preferred_element_type=F32)
        gfeat_out[pl.ds(c * BLOCK, BLOCK), :] = value.astype(BF16)
        return carry

    lax.fori_loop(0, OWN_BLOCKS, give_features, 0, unroll=2)

    wait_bytes(xy_r.at[pl.ds(0, NXY - 1)], red_recv.at[2])
    wait_bytes(xy_r.at[pl.ds(0, NXY - 1)], red_send.at[2])
    value = xy_r[0]
    for k in range(1, NXY):
        value = value + xy_r[k]
    done[core, z] = value * (float(ROOTS * 2 * NZ * NXY) ** -0.5)

    along_z(lambda pz: done.at[core, z], done.at[core, z], 3)
    wait_bytes(done.at[core, pl.ds(0, NZ - 1)], red_recv.at[3])
    wait_bytes(done.at[core, pl.ds(0, NZ - 1)], red_send.at[3])
    copy = pltpu.make_async_remote_copy(
        done.at[core], done.at[core], red_send.at[4], red_recv.at[4], device_id=mate, device_id_type=MESH
    )
    copy.start()
    copy.wait()
    gself_out[...] = done[:, :, 0:part].reshape(2 * BLOCK, BLOCK)
    gneigh_out[...] = done[:, :, part:2 * part].reshape(2 * BLOCK, BLOCK)


def make_table(tile_at):
    dest = tile_at[:, 0]
    source = tile_at[:, 1]
    tile = jnp.arange(TILES, dtype=jnp.int32)
    is_clone = (dest >= OWN_BLOCKS).astype(jnp.int32)
    key = jnp.stack([dest, is_clone * OWN_BLOCKS + source])
    order = key * TILES + tile[None, :]
    rank = jnp.sum((order[:, None, :] < order[:, :, None]).astype(jnp.int32), axis=2)
    code = jnp.stack([
        tile | (source << 8),
        tile | (jnp.where(is_clone == 1, DEST_BLOCKS, dest) << 8) | (jnp.where(is_clone == 1, dest, DEST_BLOCKS) << 16),
    ])
    same = jnp.sum(((key[:, None, :] == key[:, :, None]) & (tile[None, None, :] < tile[None, :, None])).astype(jnp.int32), axis=2)
    code = code | ((same > 0).astype(jnp.int32) << 24)
    placed = jnp.sum(jnp.where(rank[:, None, :] == tile[None, :, None], code[:, None, :], 0), axis=2)
    block = jnp.arange(2 * OWN_BLOCKS, dtype=jnp.int32)
    upto = jnp.sum((key[:, None, :] <= block[None, :, None]).astype(jnp.int32), axis=2) - 1
    has = jnp.sum((key[1][None, :] == block[:, None]).astype(jnp.int32), axis=1) > 0
    last_own = jnp.where(has, upto[1], TILES)[:OWN_BLOCKS]
    last_clone = jnp.where(has, upto[1] - OWN_BLOCKS, MOST_CLONE)[OWN_BLOCKS:]
    return jnp.concatenate([placed[0], placed[1], upto[0, :DEST_BLOCKS], last_own, last_clone])


def per_device(
    features, w_self, w_neigh, bias_vector, adjacency, tile_at, clone_root, clone_count, degrees, cotangent
):
    table = make_table(tile_at)
    live = jnp.arange(CAP, dtype=jnp.int32)[None, :] < clone_count[0][:, None]
    slots = jnp.where(live, clone_root[0], ROOTS).reshape(NZ, NY, 2, NX, CAP)
    slots = slots.transpose(0, 1, 3, 2, 4).reshape(NZ, PLANE)
    weights = jnp.concatenate([w_neigh, w_self], axis=1)
    vmem = pl.BlockSpec(memory_space=pltpu.VMEM)
    smem = pl.BlockSpec(memory_space=pltpu.SMEM)
    hbm = pl.BlockSpec(memory_space=pl.ANY)
    V = pltpu.VMEM
    part = 2 * (BLOCK // NZ)
    exchange_bufs = [
        V((NZ, NXY * CAP, BLOCK), BF16),
        V((NZ, NXY * CAP, BLOCK), BF16),
        V((NZ, NXY * CAP, BLOCK), BF16),
        V((NZ, NXY, 2 * CAP, BLOCK), BF16),
        V((NZ, NXY, 2 * CAP, BLOCK), BF16),
        V((NZ, NXY, 2 * CAP, BLOCK), BF16),
    ]
    dma = pltpu.SemaphoreType.DMA
    act, gfeat, gself, gneigh = pl.pallas_call(
        main_kernel,
        out_shape=(
            jax.ShapeDtypeStruct((OWN_BLOCKS, BLOCK, BLOCK), BF16),
            jax.ShapeDtypeStruct((ROOTS, 2 * BLOCK), BF16),
            jax.ShapeDtypeStruct((2 * BLOCK, BLOCK), F32),
            jax.ShapeDtypeStruct((2 * BLOCK, BLOCK), F32),
        ),
        in_specs=[smem, smem, hbm, vmem, vmem, hbm, vmem, vmem, vmem, vmem, vmem],
        out_specs=(vmem, vmem, vmem, vmem),
        scratch_shapes=[
            V((ROOTS, 2 * BLOCK), BF16),
            V((TILES, BLOCK, BLOCK), BF16),
            V((OWN_BLOCKS, BLOCK, BLOCK), BF16),
            V((OWN_BLOCKS, BLOCK, BLOCK), F32),
            V((TILES + 1, BLOCK, BLOCK), F32),
            V((MOST_CLONE + 1, BLOCK, BLOCK), F32),
            V((OWN_BLOCKS, BLOCK, BLOCK), F32),
            V((ROOTS + CAP, BLOCK), F32),
            V((OWN_BLOCKS, BLOCK, BLOCK), BF16),
            V((DEST_BLOCKS + 1, BLOCK, BLOCK), BF16),
            V((BLOCK, ROOTS), BF16),
            V((PLANE, BLOCK), F32),
            *exchange_bufs,
            *exchange_bufs,
            V((2, NZ, part, BLOCK), F32),
            V((NZ, part, BLOCK), F32),
            V((NZ, part, BLOCK), F32),
            V((NZ, part, BLOCK), F32),
            V((part, BLOCK), F32),
            V((NXY, part, BLOCK), F32),
            V((2, NZ, part, BLOCK), F32),
            dma((LOADS + 1,)),
            dma((2, NZ)), dma((2, NZ)), dma((2, NZ)), dma((2, NZ)), dma((2, NZ)), dma((2, NZ)),
            dma((2,)),
            dma((5,)), dma((5,)),
        ],
        compiler_params=pltpu.CompilerParams(has_side_effects=True, collective_id=1, vmem_limit_bytes=60 << 20),
        name="layer",
    )(
        table, slots.reshape(-1), features, weights, bias_vector.reshape(1, BLOCK), adjacency, slots,
        degrees.reshape(OWN_BLOCKS, BLOCK), cotangent.reshape(OWN_BLOCKS, BLOCK, BLOCK), w_self, w_neigh,
    )
    return act.reshape(ROOTS, BLOCK), gfeat, gself, gneigh


def solution(mesh):
    split = ("dom", "local")
    placed = (
        P(split, None), P(), P(), P(), P(split, None, None), P(split, None), P(split, None, None),
        P(split, None), P(split), P(split, None),
    )
    return jax.shard_map(
        per_device,
        mesh=mesh,
        in_specs=placed,
        out_specs=(P(split, None), P(split, None), P(), P()),
        check_vma=False,
    )
```

```python
import functools

import jax
import jax.numpy as jnp
from jax import lax
from jax.experimental import pallas as pl
from jax.experimental.pallas import tpu as pltpu
from jax.sharding import PartitionSpec as P

MESH = pl.DeviceIdType.MESH
F32 = jnp.float32
BF16 = jnp.bfloat16

NZ, NY, NX = 8, 4, 4
NXY = NY * NX
CAP = 8
BLOCK = 128
TILES = 192
OWN_BLOCKS = 32
CLONE_BLOCKS = 16
DEST_BLOCKS = OWN_BLOCKS + CLONE_BLOCKS
ROOTS = OWN_BLOCKS * BLOCK
MOST_OWN = TILES - CLONE_BLOCKS
MOST_CLONE = TILES - OWN_BLOCKS
PLANE = NXY * 2 * CAP
LOADS = 4

FWD, BWD, LAST_FWD, LAST_BWD = 0, 1, 2, 3
PART = 2 * BLOCK // NXY


def step_offset(i):
    return 4 + (i // 2) * (1 - i % 2) - ((i + 1) // 2) * (i % 2)


def make_table(tiles_at, out):
    across = lax.broadcasted_iota(jnp.int32, (TILES, TILES), 1)
    down = lax.broadcasted_iota(jnp.int32, (TILES, TILES), 0)

    def column(row):
        return jnp.sum(jnp.where(across == down, row, 0), axis=1, keepdims=True)

    dest = tiles_at[0:1, :]
    source = tiles_at[1:2, :]
    dest_c = column(dest)
    source_c = column(source)
    tile_c = lax.broadcasted_iota(jnp.int32, (TILES, 1), 0)
    tile = lax.broadcasted_iota(jnp.int32, (1, TILES), 1)
    is_clone = dest_c >= OWN_BLOCKS
    block = lax.broadcasted_iota(jnp.int32, (TILES, BLOCK), 1)
    key_b = source + jnp.where(dest >= OWN_BLOCKS, OWN_BLOCKS, 0)
    key_b_c = source_c + jnp.where(is_clone, OWN_BLOCKS, 0)
    code_f = tile_c + source_c * 256
    code_b = tile_c + jnp.where(is_clone, DEST_BLOCKS, dest_c) * 256 + jnp.where(is_clone, dest_c, DEST_BLOCKS) * 65536
    for at, last, key, key_c, code in ((FWD, LAST_FWD, dest, dest_c, code_f), (BWD, LAST_BWD, key_b, key_b_c, code_b)):
        before = (key * TILES + tile) < (key_c * TILES + tile_c)
        rank = jnp.sum(jnp.where(before, 1, 0), axis=1, keepdims=True)
        same = jnp.sum(jnp.where(before & (key == key_c), 1, 0), axis=1, keepdims=True)
        code = code + jnp.where(same > 0, 1 << 24, 0)
        out[at:at + 1, 0:TILES] = jnp.sum(jnp.where(rank == across, code, 0), axis=0, keepdims=True)
        upto = jnp.sum(jnp.where(key_c <= block, 1, 0), axis=0, keepdims=True) - 1
        if at == BWD:
            has = jnp.sum(jnp.where(key_c == block, 1, 0), axis=0, keepdims=True) > 0
            lane = lax.broadcasted_iota(jnp.int32, (1, BLOCK), 1)
            own = jnp.where(has, upto, TILES)
            clone = jnp.where(has, upto - OWN_BLOCKS, TILES)
            upto = jnp.where(lane < OWN_BLOCKS, own, clone)
        out[last:last + 1, 0:BLOCK] = upto


def main_kernel(
    tiles_at, root_t, count, features_h, adjacency_h, cotangent_h, bias, degrees, w_self, w_neigh,
    act_out, gfeat_out, gself_out, gneigh_out,
    table_v, table, slot_n, slot_s, slot_v, weights, cotangent, act, gfeat,
    feat, adj, proj, own, scan, total, scale, gmean, gpre, slots_t, gproj_t, rows_f,
    keep1, pass1, mate1, send1, mid1, land1,
    keep2, pass2, mate2, send2, mid2, land2,
    pieces, xy_r, sum_xy, z_r, sum_z, mate_r, done,
    load_sems, mate_send, mate_recv, xy_send, xy_recv, z_send, z_recv, own_sems,
    red_send, red_recv, out_sems,
):
    dom = lax.axis_index("dom")
    x = lax.axis_index("local")
    core = dom % 2
    zy = dom // 2
    z = zy // NY
    y = zy % NY
    xy = y * NX + x
    mate = (dom + 1 - 2 * core, x)

    def xy_peer(k):
        py = (y + k // NX) % NY
        px = (x + k % NX) % NX
        return (z * NY + py) * 2 + core, px, py * NX + px

    def z_peer(dz):
        pz = (z + dz) % NZ
        return ((pz * NY + y) * 2 + core, x), pz

    barrier = pltpu.get_barrier_semaphore()
    pl.semaphore_signal(barrier, inc=1, device_id=mate, device_id_type=MESH)
    for k in range(1, NXY):
        pdom, px, _ = xy_peer(k)
        pl.semaphore_signal(barrier, inc=1, device_id=(pdom, px), device_id_type=MESH)
    for dz in range(1, NZ):
        pl.semaphore_signal(barrier, inc=1, device_id=z_peer(dz)[0], device_id_type=MESH)

    load_feat = pltpu.make_async_copy(features_h, feat, load_sems.at[LOADS])
    load_feat.start()
    share = TILES // LOADS
    load_adj = [
        pltpu.make_async_copy(
            adjacency_h.at[pl.ds(k * share, share)], adj.at[pl.ds(k * share, share)], load_sems.at[k]
        )
        for k in range(LOADS)
    ]
    for copy in load_adj:
        copy.start()
    load_cot = pltpu.make_async_copy(cotangent_h, cotangent, load_sems.at[LOADS + 1])
    load_cot.start()

    make_table(tiles_at[...], table_v)
    live = lax.broadcasted_iota(jnp.int32, (CAP, 2 * NZ * NXY), 0) < count[...]
    slot_n[...] = jnp.where(live, root_t[...], ROOTS)
    table_copy = pltpu.make_async_copy(table_v, table, load_sems.at[LOADS + 2])
    slot_copy = pltpu.make_async_copy(slot_n, slot_s, load_sems.at[LOADS + 3])
    table_copy.start()
    slot_copy.start()

    weights[:, 0:BLOCK] = w_neigh[...]
    weights[:, BLOCK:2 * BLOCK] = w_self[...]

    load_feat.wait()
    rows = 512

    def project(i, carry):
        both = jnp.dot(feat[pl.ds(i * rows, rows), :], weights[...], preferred_element_type=F32)
        proj[pl.ds(i * (rows // BLOCK), rows // BLOCK)] = both[:, :BLOCK].astype(BF16).reshape(rows // BLOCK, BLOCK, BLOCK)
        own[pl.ds(i * (rows // BLOCK), rows // BLOCK)] = (both[:, BLOCK:] + bias[...]).reshape(rows // BLOCK, BLOCK, BLOCK)
        return carry

    lax.fori_loop(0, ROOTS // rows, project, 0, unroll=4)
    for copy in load_adj:
        copy.wait()
    table_copy.wait()
    slot_copy.wait()

    def forward(i, acc):
        code = table[FWD, i]
        tile = code & 255
        source = (code >> 8) & 255
        going = (code >> 24).astype(F32)
        acc = acc * going + jnp.dot(adj[tile], proj[source], preferred_element_type=F32)
        scan[i] = acc
        return acc

    lax.fori_loop(0, TILES, forward, jnp.zeros((BLOCK, BLOCK), F32), unroll=24)

    pl.semaphore_wait(barrier, 1 + (NXY - 1) + (NZ - 1))

    def start_swap(i, value, keep, away, back, lane):
        first = value[:, 0]
        second = value[:, 1]
        keep[i] = jnp.where(core == 0, first, second).reshape(NXY * CAP, BLOCK).astype(BF16)
        away[i] = jnp.where(core == 0, second, first).reshape(NXY * CAP, BLOCK).astype(BF16)
        swap(i, away, back, lane).start()

    def swap(i, away, back, lane):
        return pltpu.make_async_remote_copy(
            away.at[i], back.at[i], mate_send.at[lane, i], mate_recv.at[lane, i], device_id=mate, device_id_type=MESH
        )

    def start_xy(i, keep, away, back, send, mid, lane):
        swap(i, away, back, lane).wait()
        mine = keep[i].astype(F32).reshape(NXY, CAP, BLOCK)
        theirs = back[i].astype(F32).reshape(NXY, CAP, BLOCK)
        first = jnp.where(core == 0, mine, theirs)
        second = jnp.where(core == 0, theirs, mine)
        send[i] = jnp.concatenate([first, second], axis=1).astype(BF16)

        def go(k, carry):
            pdom, px, pxy = xy_peer(k)
            pltpu.make_async_remote_copy(
                send.at[i, pxy], mid.at[i, xy], xy_send.at[lane, i], xy_recv.at[lane, i],
                device_id=(pdom, px), device_id_type=MESH,
            ).start()
            return carry

        lax.fori_loop(1, NXY, go, 0)
        mid[i, xy] = send[i, xy]

    def wait_bytes(ref, sem):
        pltpu.make_async_copy(ref, ref, sem).wait()

    def z_copy(i, mid, land, lane):
        peer, _ = z_peer(step_offset(i))
        return pltpu.make_async_remote_copy(
            mid.at[i], land.at[z], z_send.at[lane, i], z_recv.at[lane, i], device_id=peer, device_id_type=MESH
        )

    def start_z(i, send, mid, land, lane):
        wait_bytes(mid.at[i, pl.ds(0, NXY - 1)], xy_recv.at[lane, i])
        wait_bytes(send.at[i, pl.ds(0, NXY - 1)], xy_send.at[lane, i])

        @pl.when(i < NZ - 1)
        def _():
            z_copy(i, mid, land, lane).start()

        @pl.when(i == NZ - 1)
        def _():
            pltpu.make_async_copy(mid.at[i], land.at[z], own_sems.at[lane]).start()

    def finish_z(i, mid, land, lane):
        @pl.when(i < NZ - 1)
        def _():
            z_copy(i, mid, land, lane).wait()

        @pl.when(i == NZ - 1)
        def _():
            pltpu.make_async_copy(mid.at[i], land.at[z], own_sems.at[lane]).wait()

        return (z + NZ - step_offset(i)) % NZ

    def send_partial(s, carry):
        pz = (z + step_offset(s)) % NZ
        first = scan[table[LAST_FWD, OWN_BLOCKS + 2 * pz]]
        second = scan[table[LAST_FWD, OWN_BLOCKS + 2 * pz + 1]]
        value = jnp.concatenate([first, second], axis=0).reshape(NY, 2, NX, CAP, BLOCK)
        value = jnp.concatenate([value[:, 0].reshape(NXY, 1, CAP, BLOCK), value[:, 1].reshape(NXY, 1, CAP, BLOCK)], axis=1)
        start_swap(s, value, keep1, pass1, mate1, 0)
        return carry

    lax.fori_loop(0, NZ, send_partial, 0)

    def send_xy(s, carry):
        start_xy(s, keep1, pass1, mate1, send1, mid1, 0)
        return carry

    lax.fori_loop(0, NZ, send_xy, 0)

    def send_z(s, carry):
        start_z(s, send1, mid1, land1, 0)
        return carry

    lax.fori_loop(0, NZ, send_z, 0)

    node = slot_n[...].astype(F32)
    high = jnp.floor(node * (1.0 / 64.0))
    low = node - high * 64.0
    both = jnp.concatenate([high, low], axis=0).astype(BF16)
    lane = lax.broadcasted_iota(jnp.int32, (2 * NZ * NXY, PLANE), 1)
    device = (lane // 64) * 8 + ((lane // 8) % 2) * 4 + (lane // 16) % 4
    down = lax.broadcasted_iota(jnp.int32, (2 * NZ * NXY, PLANE), 0)
    lane_cap = lax.broadcasted_iota(jnp.int32, (CAP, PLANE), 1) % CAP
    down_cap = lax.broadcasted_iota(jnp.int32, (CAP, PLANE), 0)
    for p in range(NZ):
        pick = jnp.where(down == device + p * 2 * NXY, 1.0, 0.0).astype(BF16)
        value = jnp.dot(both, pick, preferred_element_type=F32)
        value = value[0:CAP] * 64.0 + value[CAP:2 * CAP]
        slot_v[p:p + 1, :] = jnp.sum(jnp.where(lane_cap == down_cap, value, 0.0), axis=0, keepdims=True).astype(jnp.int32)
    def begin_total(b, carry):
        total[b] = scan[table[LAST_FWD, b]]
        inverse = 1.0 / degrees[pl.ds(b, 1), :].astype(F32)
        scale[b] = jnp.broadcast_to(inverse, (BLOCK, BLOCK)).T
        return carry

    lax.fori_loop(0, OWN_BLOCKS, begin_total, 0, unroll=2)

    def receive_plane(s, carry):
        plane = finish_z((s + NZ - 1) % NZ, mid1, land1, 0)
        arrived = land1[plane].reshape(PLANE, BLOCK)
        node = slot_v[pl.ds(plane, 1), :]
        row = lax.broadcasted_iota(jnp.int32, (BLOCK, PLANE), 0)

        def add(b, carry):
            hit = jnp.where(row == node - b * BLOCK, 1.0, 0.0).astype(BF16)
            total[b] += jnp.dot(hit, arrived, preferred_element_type=F32)
            return carry

        lax.fori_loop(0, OWN_BLOCKS, add, 0, unroll=OWN_BLOCKS)
        return carry

    lax.fori_loop(0, NZ, receive_plane, 0)
    load_cot.wait()

    def activate(b, carry):
        preact = own[b] + total[b] * scale[b]
        sig = jax.nn.sigmoid(preact)
        act[b] = (preact * sig).astype(BF16)
        full = cotangent[b].astype(F32) * sig * (1.0 + preact * (1.0 - sig))
        gpre[b] = full.astype(BF16)
        gmean[pl.ds(b * BLOCK, BLOCK), :] = full * scale[b]
        return carry

    lax.fori_loop(0, OWN_BLOCKS, activate, 0, unroll=2)
    give_act = pltpu.make_async_copy(act, act_out, out_sems.at[0])
    give_act.start()
    gmean[pl.ds(ROOTS, CAP), :] = jnp.zeros((CAP, BLOCK), F32)
    slots_t[DEST_BLOCKS] = jnp.zeros((BLOCK, BLOCK), BF16)
    scan[TILES] = jnp.zeros((BLOCK, BLOCK), F32)

    def back_own(i, acc):
        code = table[BWD, i]
        tile = code & 255
        dest = (code >> 8) & 255
        going = (code >> 24).astype(F32)
        acc = acc * going + jnp.dot(slots_t[dest], adj[tile], preferred_element_type=F32)
        scan[i] = acc
        return acc

    def gather_plane(s, carry):
        pz = (z + step_offset(s)) % NZ

        def pick(q, carry):
            d = pz * 2 * NXY + (q // 8) * 8 + (q % 2) * 4 + (q // 2) % 4
            for j in range(CAP):
                rows_f[pl.ds(q * CAP + j, 1), :] = gmean[pl.ds(slot_s[j, d], 1), :]
            return carry

        lax.fori_loop(0, 2 * NXY, pick, 0, unroll=16)
        start_swap(s, rows_f[...].reshape(NXY, 2, CAP, BLOCK), keep2, pass2, mate2, 1)
        return carry

    def send_back(s, carry):
        gather_plane(s, 0)

        @pl.when(s >= 2)
        def _():
            start_xy(s - 2, keep2, pass2, mate2, send2, mid2, 1)

        @pl.when(s >= 5)
        def _():
            start_z(s - 5, send2, mid2, land2, 1)

        return carry

    lax.fori_loop(0, NZ, send_back, 0)
    start_xy(NZ - 2, keep2, pass2, mate2, send2, mid2, 1)

    def transpose(b, carry):
        at = pl.ds(pl.multiple_of(b * BLOCK, BLOCK), BLOCK)
        gproj_t[:, at] = gpre[b].astype(F32).T.astype(BF16)
        slots_t[b] = gmean[pl.ds(b * BLOCK, BLOCK), :].T.astype(BF16)
        return carry

    lax.fori_loop(0, OWN_BLOCKS // 2, transpose, 0, unroll=2)
    start_xy(NZ - 1, keep2, pass2, mate2, send2, mid2, 1)
    start_z(NZ - 5, send2, mid2, land2, 1)
    start_z(NZ - 4, send2, mid2, land2, 1)
    lax.fori_loop(OWN_BLOCKS // 2, OWN_BLOCKS, transpose, 0, unroll=2)
    start_z(NZ - 3, send2, mid2, land2, 1)
    start_z(NZ - 2, send2, mid2, land2, 1)
    start_z(NZ - 1, send2, mid2, land2, 1)
    gself = jnp.dot(gproj_t[...], feat[...], preferred_element_type=F32).T

    def wait_both(ref, lane, k):
        wait_bytes(ref, red_recv.at[lane, k])
        wait_bytes(ref, red_send.at[lane, k])

    def around_xy(src, dst, lane, k):
        def go(j, carry):
            pdom, px, pxy = xy_peer(j)
            pltpu.make_async_remote_copy(
                src(pxy), dst, red_send.at[lane, k], red_recv.at[lane, k],
                device_id=(pdom, px), device_id_type=MESH,
            ).start()
            return carry

        lax.fori_loop(1, NXY, go, 0)

    def swap_sums(lane):
        return pltpu.make_async_remote_copy(
            sum_z.at[lane], mate_r.at[lane], red_send.at[lane, 2], red_recv.at[lane, 2],
            device_id=mate, device_id_type=MESH,
        )

    def reduce_0(value, lane):
        pieces[lane] = value.reshape(NXY, PART, BLOCK)
        around_xy(lambda pxy: pieces.at[lane, pxy], xy_r.at[lane, xy], lane, 0)
        xy_r[lane, xy] = pieces[lane, xy]

    def reduce_1(lane):
        wait_both(xy_r.at[lane, pl.ds(0, NXY - 1)], lane, 0)
        value = xy_r[lane, 0]
        for k in range(1, NXY):
            value = value + xy_r[lane, k]
        sum_xy[lane] = value

        def go(dz, carry):
            peer, _ = z_peer(dz)
            pltpu.make_async_remote_copy(
                sum_xy.at[lane], z_r.at[lane, z], red_send.at[lane, 1], red_recv.at[lane, 1],
                device_id=peer, device_id_type=MESH,
            ).start()
            return carry

        lax.fori_loop(1, NZ, go, 0)
        z_r[lane, z] = value

    def reduce_2(lane):
        wait_both(z_r.at[lane, pl.ds(0, NZ - 1)], lane, 1)
        value = z_r[lane, 0]
        for k in range(1, NZ):
            value = value + z_r[lane, k]
        sum_z[lane] = value
        swap_sums(lane).start()

    def reduce_3(lane):
        swap_sums(lane).wait()
        done[lane, xy] = (sum_z[lane] + mate_r[lane]) * (float(ROOTS * 2 * NZ * NXY) ** -0.5)
        around_xy(lambda pxy: done.at[lane, xy], done.at[lane, xy], lane, 3)

    def reduce_4(lane, out):
        wait_both(done.at[lane, pl.ds(0, NXY - 1)], lane, 3)
        out[...] = done[lane].reshape(2 * BLOCK, BLOCK)

    reduce_0(gself, 0)
    lax.fori_loop(0, MOST_OWN, back_own, jnp.zeros((BLOCK, BLOCK), F32), unroll=22)

    def keep_own(c, carry):
        total[c] = scan[table[LAST_BWD, c]]
        return carry

    lax.fori_loop(0, OWN_BLOCKS, keep_own, 0, unroll=4)

    def arrived_back(s, carry):
        plane = finish_z((s + NZ - 1) % NZ, mid2, land2, 1)
        value = land2[plane].astype(F32).reshape(NY, NX, 2, CAP, BLOCK)
        value = jnp.concatenate(
            [value[:, :, 0].reshape(NY, 1, NX, CAP, BLOCK), value[:, :, 1].reshape(NY, 1, NX, CAP, BLOCK)], axis=1
        ).reshape(2, BLOCK, BLOCK)
        slots_t[OWN_BLOCKS + 2 * plane] = value[0].T.astype(BF16)
        slots_t[OWN_BLOCKS + 2 * plane + 1] = value[1].T.astype(BF16)
        return carry

    lax.fori_loop(0, NZ, arrived_back, 0)
    reduce_1(0)

    def back_clone(i, acc):
        code = table[BWD, OWN_BLOCKS + i]
        tile = code & 255
        dest = (code >> 16) & 255
        going = (code >> 24).astype(F32)
        acc = acc * going + jnp.dot(slots_t[dest], adj[tile], preferred_element_type=F32)
        scan[i] = acc
        return acc

    lax.fori_loop(0, MOST_CLONE, back_clone, jnp.zeros((BLOCK, BLOCK), F32), unroll=20)

    def gather_proj(c, carry):
        value = total[c] + scan[table[LAST_BWD, OWN_BLOCKS + c]]
        at = pl.ds(pl.multiple_of(c * BLOCK, BLOCK), BLOCK)
        gproj_t[:, at] = value.astype(BF16)
        return carry

    lax.fori_loop(0, OWN_BLOCKS, gather_proj, 0, unroll=4)
    reduce_2(0)
    gneigh = jnp.dot(gproj_t[...], feat[...], preferred_element_type=F32).T

    reduce_0(gneigh, 1)
    reduce_3(0)

    def give_features(c, carry):
        at = pl.ds(pl.multiple_of(c * BLOCK, BLOCK), BLOCK)
        value = lax.dot_general(gpre[c], w_self[...], (((1,), (1,)), ((), ())), preferred_element_type=F32)
        value += lax.dot_general(gproj_t[:, at], w_neigh[...], (((0,), (1,)), ((), ())), preferred_element_type=F32)
        gfeat[pl.ds(c * BLOCK, BLOCK), :] = value.astype(BF16)
        return carry

    lax.fori_loop(0, OWN_BLOCKS // 4, give_features, 0, unroll=8)
    reduce_1(1)
    lax.fori_loop(OWN_BLOCKS // 4, OWN_BLOCKS // 2, give_features, 0, unroll=8)
    reduce_2(1)
    lax.fori_loop(OWN_BLOCKS // 2, OWN_BLOCKS // 4 * 3, give_features, 0, unroll=8)
    reduce_3(1)
    lax.fori_loop(OWN_BLOCKS // 4 * 3, OWN_BLOCKS, give_features, 0, unroll=8)
    give_feat = pltpu.make_async_copy(gfeat, gfeat_out, out_sems.at[1])
    give_feat.start()
    reduce_4(0, gself_out)
    reduce_4(1, gneigh_out)
    give_act.wait()
    give_feat.wait()


def finish_kernel(act, gfeat, gself, gneigh, act_out, gfeat_out, gself_out, gneigh_out, sems):
    copies = [
        pltpu.make_async_copy(src, dst, sems.at[k])
        for k, (src, dst) in enumerate(
            ((gfeat, gfeat_out), (act, act_out), (gself, gself_out), (gneigh, gneigh_out))
        )
    ]
    for copy in copies:
        copy.start()
    for copy in copies:
        copy.wait()


def per_device(
    features, w_self, w_neigh, bias_vector, adjacency, tile_at, clone_root, clone_count, degrees, cotangent
):
    vmem = pl.BlockSpec(memory_space=pltpu.VMEM)
    hbm = pl.BlockSpec(memory_space=pl.ANY)
    V = pltpu.VMEM
    exchange_bufs = [
        V((NZ, NXY * CAP, BLOCK), BF16),
        V((NZ, NXY * CAP, BLOCK), BF16),
        V((NZ, NXY * CAP, BLOCK), BF16),
        V((NZ, NXY, 2 * CAP, BLOCK), BF16),
        V((NZ, NXY, 2 * CAP, BLOCK), BF16),
        V((NZ, NXY, 2 * CAP, BLOCK), BF16),
    ]
    dma = pltpu.SemaphoreType.DMA
    outs = (
        jax.ShapeDtypeStruct((OWN_BLOCKS, BLOCK, BLOCK), BF16),
        jax.ShapeDtypeStruct((ROOTS, 2 * BLOCK), BF16),
        jax.ShapeDtypeStruct((2 * BLOCK, BLOCK), F32),
        jax.ShapeDtypeStruct((2 * BLOCK, BLOCK), F32),
    )
    results = pl.pallas_call(
        main_kernel,
        out_shape=outs,
        in_specs=[vmem, vmem, vmem, hbm, hbm, hbm, vmem, vmem, vmem, vmem],
        out_specs=(hbm, hbm, vmem, vmem),
        scratch_shapes=[
            V((8, 256), jnp.int32),
            pltpu.SMEM((8, 256), jnp.int32),
            V((CAP, 2 * NZ * NXY), jnp.int32),
            pltpu.SMEM((CAP, 2 * NZ * NXY), jnp.int32),
            V((NZ, PLANE), jnp.int32),
            V((2 * BLOCK, 2 * BLOCK), BF16),
            V((OWN_BLOCKS, BLOCK, BLOCK), BF16),
            V((OWN_BLOCKS, BLOCK, BLOCK), BF16),
            V((ROOTS, 2 * BLOCK), BF16),
            V((ROOTS, 2 * BLOCK), BF16),
            V((TILES, BLOCK, BLOCK), BF16),
            V((OWN_BLOCKS, BLOCK, BLOCK), BF16),
            V((OWN_BLOCKS, BLOCK, BLOCK), F32),
            V((TILES + 1, BLOCK, BLOCK), F32),
            V((OWN_BLOCKS, BLOCK, BLOCK), F32),
            V((OWN_BLOCKS, BLOCK, BLOCK), F32),
            V((ROOTS + CAP, BLOCK), F32),
            V((OWN_BLOCKS, BLOCK, BLOCK), BF16),
            V((DEST_BLOCKS + 1, BLOCK, BLOCK), BF16),
            V((BLOCK, ROOTS), BF16),
            V((PLANE, BLOCK), F32),
            *exchange_bufs,
            *exchange_bufs,
            V((2, NXY, PART, BLOCK), F32),
            V((2, NXY, PART, BLOCK), F32),
            V((2, PART, BLOCK), F32),
            V((2, NZ, PART, BLOCK), F32),
            V((2, PART, BLOCK), F32),
            V((2, PART, BLOCK), F32),
            V((2, NXY, PART, BLOCK), F32),
            dma((LOADS + 4,)),
            dma((2, NZ)), dma((2, NZ)), dma((2, NZ)), dma((2, NZ)), dma((2, NZ)), dma((2, NZ)),
            dma((2,)),
            dma((2, 4)), dma((2, 4)), dma((2,)),
        ],
        compiler_params=pltpu.CompilerParams(has_side_effects=True, collective_id=1, vmem_limit_bytes=60 << 20),
        name="layer",
    )(
        tile_at.T, clone_root[0].T, clone_count, features, adjacency, cotangent.reshape(OWN_BLOCKS, BLOCK, BLOCK),
        bias_vector.reshape(1, BLOCK), degrees.reshape(OWN_BLOCKS, BLOCK), w_self, w_neigh,
    )
    act, gfeat, gself, gneigh = pl.pallas_call(
        finish_kernel,
        out_shape=outs,
        in_specs=[vmem] * 4,
        out_specs=(hbm,) * 4,
        scratch_shapes=[dma((4,))],
        name="finish",
    )(*results)
    return act.reshape(ROOTS, BLOCK), gfeat, gself, gneigh


def solution(mesh):
    split = ("dom", "local")
    placed = (
        P(split, None), P(), P(), P(), P(split, None, None), P(split, None), P(split, None, None),
        P(split, None), P(split), P(split, None),
    )
    return jax.shard_map(
        per_device,
        mesh=mesh,
        in_specs=placed,
        out_specs=(P(split, None), P(split, None), P(), P()),
        check_vma=False,
    )
```

```python
import functools

import jax
import jax.numpy as jnp
from jax import lax
from jax.experimental import pallas as pl
from jax.experimental.pallas import tpu as pltpu
from jax.sharding import PartitionSpec as P

MESH = pl.DeviceIdType.MESH
F32 = jnp.float32
BF16 = jnp.bfloat16

NZ, NY, NX = 8, 4, 4
NXY = NY * NX
CAP = 8
BLOCK = 128
TILES = 192
OWN_BLOCKS = 32
CLONE_BLOCKS = 16
DEST_BLOCKS = OWN_BLOCKS + CLONE_BLOCKS
ROOTS = OWN_BLOCKS * BLOCK
MOST_OWN = TILES - CLONE_BLOCKS
MOST_CLONE = TILES - OWN_BLOCKS
PLANE = NXY * 2 * CAP
LOADS = 4

FWD, BWD, LAST_FWD, LAST_BWD = 0, 1, 2, 3
PART = 2 * BLOCK // NXY


def step_offset(i):
    return 4 + (i // 2) * (1 - i % 2) - ((i + 1) // 2) * (i % 2)


def make_table(tiles_at, out):
    across = lax.broadcasted_iota(jnp.int32, (TILES, TILES), 1)
    down = lax.broadcasted_iota(jnp.int32, (TILES, TILES), 0)

    def column(row):
        return jnp.sum(jnp.where(across == down, row, 0), axis=1, keepdims=True)

    dest = tiles_at[0:1, :]
    source = tiles_at[1:2, :]
    dest_c = column(dest)
    source_c = column(source)
    tile_c = lax.broadcasted_iota(jnp.int32, (TILES, 1), 0)
    tile = lax.broadcasted_iota(jnp.int32, (1, TILES), 1)
    is_clone = dest_c >= OWN_BLOCKS
    block = lax.broadcasted_iota(jnp.int32, (TILES, BLOCK), 1)
    key_b = source + jnp.where(dest >= OWN_BLOCKS, OWN_BLOCKS, 0)
    key_b_c = source_c + jnp.where(is_clone, OWN_BLOCKS, 0)
    code_f = tile_c + source_c * 256
    code_b = tile_c + jnp.where(is_clone, DEST_BLOCKS, dest_c) * 256 + jnp.where(is_clone, dest_c, DEST_BLOCKS) * 65536
    for at, last, key, key_c, code in ((FWD, LAST_FWD, dest, dest_c, code_f), (BWD, LAST_BWD, key_b, key_b_c, code_b)):
        before = (key * TILES + tile) < (key_c * TILES + tile_c)
        rank = jnp.sum(jnp.where(before, 1, 0), axis=1, keepdims=True)
        same = jnp.sum(jnp.where(before & (key == key_c), 1, 0), axis=1, keepdims=True)
        code = code + jnp.where(same > 0, 1 << 24, 0)
        out[at:at + 1, 0:TILES] = jnp.sum(jnp.where(rank == across, code, 0), axis=0, keepdims=True)
        upto = jnp.sum(jnp.where(key_c <= block, 1, 0), axis=0, keepdims=True) - 1
        if at == BWD:
            has = jnp.sum(jnp.where(key_c == block, 1, 0), axis=0, keepdims=True) > 0
            lane = lax.broadcasted_iota(jnp.int32, (1, BLOCK), 1)
            own = jnp.where(has, upto, TILES)
            clone = jnp.where(has, upto - OWN_BLOCKS, TILES)
            upto = jnp.where(lane < OWN_BLOCKS, own, clone)
        out[last:last + 1, 0:BLOCK] = upto


def main_kernel(
    tiles_at, root_t, count, features_h, adjacency_h, cotangent_h, bias, degrees, w_self, w_neigh,
    act_out, gfeat_out, gself_out, gneigh_out,
    table_v, table, slot_n, slot_s, slot_v, weights, cotangent, act, gfeat,
    feat, adj, proj, own, scan, total, scale, gmean, gpre, slots_t, gproj_t, rows_f,
    keep1, pass1, mate1, send1, mid1, land1,
    keep2, pass2, mate2, send2, mid2, land2,
    pieces, xy_r, sum_xy, z_r, sum_z, mate_r, done,
    load_sems, mate_send, mate_recv, xy_send, xy_recv, z_send, z_recv, own_sems,
    red_send, red_recv, out_sems,
):
    dom = lax.axis_index("dom")
    x = lax.axis_index("local")
    core = dom % 2
    zy = dom // 2
    z = zy // NY
    y = zy % NY
    xy = y * NX + x
    mate = (dom + 1 - 2 * core, x)

    def xy_peer(k):
        py = lax.rem(y + k // NX, NY)
        px = lax.rem(x + k % NX, NX)
        return (z * NY + py) * 2 + core, px, py * NX + px

    def z_peer(dz):
        pz = lax.rem(z + dz, NZ)
        return ((pz * NY + y) * 2 + core, x), pz

    barrier = pltpu.get_barrier_semaphore()
    pl.semaphore_signal(barrier, inc=1, device_id=mate, device_id_type=MESH)
    for k in range(1, NXY):
        pdom, px, _ = xy_peer(k)
        pl.semaphore_signal(barrier, inc=1, device_id=(pdom, px), device_id_type=MESH)
    for dz in range(1, NZ):
        pl.semaphore_signal(barrier, inc=1, device_id=z_peer(dz)[0], device_id_type=MESH)

    load_feat = pltpu.make_async_copy(features_h, feat, load_sems.at[LOADS])
    load_feat.start()
    share = TILES // LOADS
    load_adj = [
        pltpu.make_async_copy(
            adjacency_h.at[pl.ds(k * share, share)], adj.at[pl.ds(k * share, share)], load_sems.at[k]
        )
        for k in range(LOADS)
    ]
    for copy in load_adj:
        copy.start()
    load_cot = pltpu.make_async_copy(cotangent_h, cotangent, load_sems.at[LOADS + 1])
    load_cot.start()

    make_table(tiles_at[...], table_v)
    live = lax.broadcasted_iota(jnp.int32, (CAP, 2 * NZ * NXY), 0) < count[...]
    slot_n[...] = jnp.where(live, root_t[...], ROOTS)
    table_copy = pltpu.make_async_copy(table_v, table, load_sems.at[LOADS + 2])
    slot_copy = pltpu.make_async_copy(slot_n, slot_s, load_sems.at[LOADS + 3])
    table_copy.start()
    slot_copy.start()

    weights[:, 0:BLOCK] = w_neigh[...]
    weights[:, BLOCK:2 * BLOCK] = w_self[...]

    load_feat.wait()
    rows = 512

    def project(i, carry):
        both = jnp.dot(feat[pl.ds(i * rows, rows), :], weights[...], preferred_element_type=F32)
        proj[pl.ds(i * (rows // BLOCK), rows // BLOCK)] = both[:, :BLOCK].astype(BF16).reshape(rows // BLOCK, BLOCK, BLOCK)
        own[pl.ds(i * (rows // BLOCK), rows // BLOCK)] = (both[:, BLOCK:] + bias[...]).reshape(rows // BLOCK, BLOCK, BLOCK)
        return carry

    lax.fori_loop(0, ROOTS // rows, project, 0, unroll=4)
    for copy in load_adj:
        copy.wait()
    table_copy.wait()
    slot_copy.wait()

    def forward(i, acc):
        code = table[FWD, i]
        tile = code & 255
        source = (code >> 8) & 255
        going = (code >> 24).astype(F32)
        acc = acc * going + jnp.dot(adj[tile], proj[source], preferred_element_type=F32)
        scan[i] = acc
        return acc

    lax.fori_loop(0, TILES, forward, jnp.zeros((BLOCK, BLOCK), F32), unroll=24)

    pl.semaphore_wait(barrier, 1 + (NXY - 1) + (NZ - 1))

    def start_swap(i, value, keep, away, back, lane):
        first = value[:, 0]
        second = value[:, 1]
        keep[i] = jnp.where(core == 0, first, second).reshape(NXY * CAP, BLOCK).astype(BF16)
        away[i] = jnp.where(core == 0, second, first).reshape(NXY * CAP, BLOCK).astype(BF16)
        swap(i, away, back, lane).start()

    def swap(i, away, back, lane):
        return pltpu.make_async_remote_copy(
            away.at[i], back.at[i], mate_send.at[lane, i], mate_recv.at[lane, i], device_id=mate, device_id_type=MESH
        )

    def start_xy(i, keep, away, back, send, mid, lane):
        swap(i, away, back, lane).wait()
        mine = keep[i].astype(F32).reshape(NXY, CAP, BLOCK)
        theirs = back[i].astype(F32).reshape(NXY, CAP, BLOCK)
        first = jnp.where(core == 0, mine, theirs)
        second = jnp.where(core == 0, theirs, mine)
        send[i] = jnp.concatenate([first, second], axis=1).astype(BF16)

        for k in range(1, NXY):
            pdom, px, pxy = xy_peer(k)
            pltpu.make_async_remote_copy(
                send.at[i, pxy], mid.at[i, xy], xy_send.at[lane, i], xy_recv.at[lane, i],
                device_id=(pdom, px), device_id_type=MESH,
            ).start()
        mid[i, xy] = send[i, xy]

    def wait_bytes(ref, sem):
        pltpu.make_async_copy(ref, ref, sem).wait()

    def z_copy(i, mid, land, lane):
        peer, _ = z_peer(step_offset(i))
        return pltpu.make_async_remote_copy(
            mid.at[i], land.at[z], z_send.at[lane, i], z_recv.at[lane, i], device_id=peer, device_id_type=MESH
        )

    def start_z(i, send, mid, land, lane):
        wait_bytes(mid.at[i, pl.ds(0, NXY - 1)], xy_recv.at[lane, i])
        wait_bytes(send.at[i, pl.ds(0, NXY - 1)], xy_send.at[lane, i])

        if isinstance(i, int) and i < NZ - 1:
            z_copy(i, mid, land, lane).start()
        elif isinstance(i, int):
            pltpu.make_async_copy(mid.at[i], land.at[z], own_sems.at[lane]).start()
        else:
            @pl.when(i < NZ - 1)
            def _():
                z_copy(i, mid, land, lane).start()

            @pl.when(i == NZ - 1)
            def _():
                pltpu.make_async_copy(mid.at[i], land.at[z], own_sems.at[lane]).start()

    def finish_z(i, mid, land, lane):
        @pl.when(i < NZ - 1)
        def _():
            z_copy(i, mid, land, lane).wait()

        @pl.when(i == NZ - 1)
        def _():
            pltpu.make_async_copy(mid.at[i], land.at[z], own_sems.at[lane]).wait()

        return (z + NZ - step_offset(i)) % NZ

    def send_partial(s, carry):
        pz = (z + step_offset(s)) % NZ
        first = scan[table[LAST_FWD, OWN_BLOCKS + 2 * pz]]
        second = scan[table[LAST_FWD, OWN_BLOCKS + 2 * pz + 1]]
        value = jnp.concatenate([first, second], axis=0).reshape(NY, 2, NX, CAP, BLOCK)
        value = jnp.concatenate([value[:, 0].reshape(NXY, 1, CAP, BLOCK), value[:, 1].reshape(NXY, 1, CAP, BLOCK)], axis=1)
        start_swap(s, value, keep1, pass1, mate1, 0)
        return carry

    lax.fori_loop(0, NZ, send_partial, 0)

    def send_xy(s, carry):
        start_xy(s, keep1, pass1, mate1, send1, mid1, 0)
        return carry

    lax.fori_loop(0, NZ, send_xy, 0)

    def send_z(s, carry):
        start_z(s, send1, mid1, land1, 0)
        return carry

    lax.fori_loop(0, NZ, send_z, 0)

    node = slot_n[...].astype(F32)
    high = jnp.floor(node * (1.0 / 64.0))
    low = node - high * 64.0
    both = jnp.concatenate([high, low], axis=0).astype(BF16)
    lane = lax.broadcasted_iota(jnp.int32, (2 * NZ * NXY, PLANE), 1)
    device = (lane // 64) * 8 + ((lane // 8) % 2) * 4 + (lane // 16) % 4
    down = lax.broadcasted_iota(jnp.int32, (2 * NZ * NXY, PLANE), 0)
    lane_cap = lax.broadcasted_iota(jnp.int32, (CAP, PLANE), 1) % CAP
    down_cap = lax.broadcasted_iota(jnp.int32, (CAP, PLANE), 0)
    for p in range(NZ):
        pick = jnp.where(down == device + p * 2 * NXY, 1.0, 0.0).astype(BF16)
        value = jnp.dot(both, pick, preferred_element_type=F32)
        value = value[0:CAP] * 64.0 + value[CAP:2 * CAP]
        slot_v[p:p + 1, :] = jnp.sum(jnp.where(lane_cap == down_cap, value, 0.0), axis=0, keepdims=True).astype(jnp.int32)
    def begin_total(b, carry):
        total[b] = scan[table[LAST_FWD, b]]
        inverse = 1.0 / degrees[pl.ds(b, 1), :].astype(F32)
        scale[b] = jnp.broadcast_to(inverse, (BLOCK, BLOCK)).T
        return carry

    lax.fori_loop(0, OWN_BLOCKS, begin_total, 0, unroll=2)

    def receive_plane(s, carry):
        plane = finish_z((s + NZ - 1) % NZ, mid1, land1, 0)
        arrived = land1[plane].reshape(PLANE, BLOCK)
        node = slot_v[pl.ds(plane, 1), :]
        row = lax.broadcasted_iota(jnp.int32, (BLOCK, PLANE), 0)

        def add(b, carry):
            hit = jnp.where(row == node - b * BLOCK, 1.0, 0.0).astype(BF16)
            total[b] += jnp.dot(hit, arrived, preferred_element_type=F32)
            return carry

        lax.fori_loop(0, OWN_BLOCKS, add, 0, unroll=OWN_BLOCKS)
        return carry

    lax.fori_loop(0, NZ, receive_plane, 0)
    load_cot.wait()

    def activate(b, carry):
        preact = own[b] + total[b] * scale[b]
        sig = jax.nn.sigmoid(preact)
        act[b] = (preact * sig).astype(BF16)
        full = cotangent[b].astype(F32) * sig * (1.0 + preact * (1.0 - sig))
        gpre[b] = full.astype(BF16)
        gmean[pl.ds(b * BLOCK, BLOCK), :] = full * scale[b]
        return carry

    lax.fori_loop(0, OWN_BLOCKS, activate, 0, unroll=2)
    give_act = pltpu.make_async_copy(act, act_out, out_sems.at[0])
    give_act.start()
    gmean[pl.ds(ROOTS, CAP), :] = jnp.zeros((CAP, BLOCK), F32)
    slots_t[DEST_BLOCKS] = jnp.zeros((BLOCK, BLOCK), BF16)
    scan[TILES] = jnp.zeros((BLOCK, BLOCK), F32)

    def back_own(i, acc):
        code = table[BWD, i]
        tile = code & 255
        dest = (code >> 8) & 255
        going = (code >> 24).astype(F32)
        acc = acc * going + jnp.dot(slots_t[dest], adj[tile], preferred_element_type=F32)
        scan[i] = acc
        return acc

    def gather_plane(s, carry):
        pz = (z + step_offset(s)) % NZ

        for q in range(2 * NXY):
            d = pz * 2 * NXY + (q // 8) * 8 + (q % 2) * 4 + (q // 2) % 4
            for j in range(CAP):
                rows_f[q * CAP + j:q * CAP + j + 1, :] = gmean[pl.ds(slot_s[j, d], 1), :]
        start_swap(s, rows_f[...].reshape(NXY, 2, CAP, BLOCK), keep2, pass2, mate2, 1)
        return carry

    def send_back(s, carry):
        gather_plane(s, 0)

        @pl.when(s >= 3)
        def _():
            start_xy(s - 3, keep2, pass2, mate2, send2, mid2, 1)

        return carry

    lax.fori_loop(0, NZ, send_back, 0)
    def transpose(b, carry):
        at = pl.ds(pl.multiple_of(b * BLOCK, BLOCK), BLOCK)
        gproj_t[:, at] = gpre[b].astype(F32).T.astype(BF16)
        slots_t[b] = gmean[pl.ds(b * BLOCK, BLOCK), :].T.astype(BF16)
        return carry

    for k in range(3):
        start_xy(NZ - 3 + k, keep2, pass2, mate2, send2, mid2, 1)
        start_z(k, send2, mid2, land2, 1)
    lax.fori_loop(0, OWN_BLOCKS // 2, transpose, 0, unroll=4)
    start_z(3, send2, mid2, land2, 1)
    start_z(4, send2, mid2, land2, 1)
    lax.fori_loop(OWN_BLOCKS // 2, OWN_BLOCKS, transpose, 0, unroll=4)
    start_z(5, send2, mid2, land2, 1)
    start_z(6, send2, mid2, land2, 1)
    start_z(7, send2, mid2, land2, 1)
    gself = jnp.dot(gproj_t[...], feat[...], preferred_element_type=F32).T

    def wait_both(ref, lane, k):
        wait_bytes(ref, red_recv.at[lane, k])
        wait_bytes(ref, red_send.at[lane, k])

    def around_xy(src, dst, lane, k):
        for j in range(1, NXY):
            pdom, px, pxy = xy_peer(j)
            pltpu.make_async_remote_copy(
                src(pxy), dst, red_send.at[lane, k], red_recv.at[lane, k],
                device_id=(pdom, px), device_id_type=MESH,
            ).start()

    def swap_sums(lane):
        return pltpu.make_async_remote_copy(
            sum_z.at[lane], mate_r.at[lane], red_send.at[lane, 2], red_recv.at[lane, 2],
            device_id=mate, device_id_type=MESH,
        )

    def reduce_0(value, lane):
        pieces[lane] = value.reshape(NXY, PART, BLOCK)
        around_xy(lambda pxy: pieces.at[lane, pxy], xy_r.at[lane, xy], lane, 0)
        xy_r[lane, xy] = pieces[lane, xy]

    def reduce_1(lane):
        wait_both(xy_r.at[lane, pl.ds(0, NXY - 1)], lane, 0)
        value = xy_r[lane, 0]
        for k in range(1, NXY):
            value = value + xy_r[lane, k]
        sum_xy[lane] = value

        for dz in range(1, NZ):
            peer, _ = z_peer(dz)
            pltpu.make_async_remote_copy(
                sum_xy.at[lane], z_r.at[lane, z], red_send.at[lane, 1], red_recv.at[lane, 1],
                device_id=peer, device_id_type=MESH,
            ).start()
        z_r[lane, z] = value

    def reduce_2(lane):
        wait_both(z_r.at[lane, pl.ds(0, NZ - 1)], lane, 1)
        value = z_r[lane, 0]
        for k in range(1, NZ):
            value = value + z_r[lane, k]
        sum_z[lane] = value
        swap_sums(lane).start()

    def reduce_3(lane):
        swap_sums(lane).wait()
        done[lane, xy] = (sum_z[lane] + mate_r[lane]) * (float(ROOTS * 2 * NZ * NXY) ** -0.5)
        around_xy(lambda pxy: done.at[lane, xy], done.at[lane, xy], lane, 3)

    def reduce_4(lane, out):
        wait_both(done.at[lane, pl.ds(0, NXY - 1)], lane, 3)
        out[...] = done[lane].reshape(2 * BLOCK, BLOCK)

    reduce_0(gself, 0)
    lax.fori_loop(0, MOST_OWN, back_own, jnp.zeros((BLOCK, BLOCK), F32), unroll=22)

    def keep_own(c, carry):
        total[c] = scan[table[LAST_BWD, c]]
        return carry

    lax.fori_loop(0, OWN_BLOCKS, keep_own, 0, unroll=4)

    def arrived_back(s, carry):
        plane = finish_z((s + NZ - 1) % NZ, mid2, land2, 1)
        value = land2[plane].astype(F32).reshape(NY, NX, 2, CAP, BLOCK)
        value = jnp.concatenate(
            [value[:, :, 0].reshape(NY, 1, NX, CAP, BLOCK), value[:, :, 1].reshape(NY, 1, NX, CAP, BLOCK)], axis=1
        ).reshape(2, BLOCK, BLOCK)
        slots_t[OWN_BLOCKS + 2 * plane] = value[0].T.astype(BF16)
        slots_t[OWN_BLOCKS + 2 * plane + 1] = value[1].T.astype(BF16)
        return carry

    lax.fori_loop(0, NZ, arrived_back, 0)
    reduce_1(0)

    def back_clone(i, acc):
        code = table[BWD, OWN_BLOCKS + i]
        tile = code & 255
        dest = (code >> 16) & 255
        going = (code >> 24).astype(F32)
        acc = acc * going + jnp.dot(slots_t[dest], adj[tile], preferred_element_type=F32)
        scan[i] = acc
        return acc

    lax.fori_loop(0, MOST_CLONE, back_clone, jnp.zeros((BLOCK, BLOCK), F32), unroll=20)

    def gather_proj(c, carry):
        value = total[c] + scan[table[LAST_BWD, OWN_BLOCKS + c]]
        at = pl.ds(pl.multiple_of(c * BLOCK, BLOCK), BLOCK)
        gproj_t[:, at] = value.astype(BF16)
        return carry

    lax.fori_loop(0, OWN_BLOCKS, gather_proj, 0, unroll=4)
    reduce_2(0)
    gneigh = jnp.dot(gproj_t[...], feat[...], preferred_element_type=F32).T

    reduce_0(gneigh, 1)
    reduce_3(0)

    def give_features(c, carry):
        at = pl.ds(pl.multiple_of(c * BLOCK, BLOCK), BLOCK)
        value = lax.dot_general(gpre[c], w_self[...], (((1,), (1,)), ((), ())), preferred_element_type=F32)
        value += lax.dot_general(gproj_t[:, at], w_neigh[...], (((0,), (1,)), ((), ())), preferred_element_type=F32)
        gfeat[pl.ds(c * BLOCK, BLOCK), :] = value.astype(BF16)
        return carry

    lax.fori_loop(0, OWN_BLOCKS // 4, give_features, 0, unroll=8)
    reduce_1(1)
    lax.fori_loop(OWN_BLOCKS // 4, OWN_BLOCKS // 2, give_features, 0, unroll=8)
    reduce_2(1)
    lax.fori_loop(OWN_BLOCKS // 2, OWN_BLOCKS // 4 * 3, give_features, 0, unroll=8)
    reduce_3(1)
    lax.fori_loop(OWN_BLOCKS // 4 * 3, OWN_BLOCKS, give_features, 0, unroll=8)
    give_feat = pltpu.make_async_copy(gfeat, gfeat_out, out_sems.at[1])
    give_feat.start()
    reduce_4(0, gself_out)
    reduce_4(1, gneigh_out)
    give_act.wait()
    give_feat.wait()


def finish_kernel(act, gfeat, gself, gneigh, act_out, gfeat_out, gself_out, gneigh_out, act_v, gfeat_v, gself_v, gneigh_v, load, give):
    copies = []
    for src, mid, dst, cuts in (
        (gfeat, gfeat_v, gfeat_out, 4), (act, act_v, act_out, 2), (gself, gself_v, gself_out, 1), (gneigh, gneigh_v, gneigh_out, 1)
    ):
        rows = src.shape[0] // cuts
        for k in range(cuts):
            at = pl.ds(k * rows, rows)
            n = len(copies)
            copies.append((
                pltpu.make_async_copy(src.at[at], mid.at[at], load.at[n]),
                pltpu.make_async_copy(mid.at[at], dst.at[at], give.at[n]),
            ))
    for into, _ in copies:
        into.start()
    for into, out in copies:
        into.wait()
        out.start()
    for _, out in copies:
        out.wait()


def per_device(
    features, w_self, w_neigh, bias_vector, adjacency, tile_at, clone_root, clone_count, degrees, cotangent
):
    vmem = pl.BlockSpec(memory_space=pltpu.VMEM)
    hbm = pl.BlockSpec(memory_space=pl.ANY)
    V = pltpu.VMEM
    exchange_bufs = [
        V((NZ, NXY * CAP, BLOCK), BF16),
        V((NZ, NXY * CAP, BLOCK), BF16),
        V((NZ, NXY * CAP, BLOCK), BF16),
        V((NZ, NXY, 2 * CAP, BLOCK), BF16),
        V((NZ, NXY, 2 * CAP, BLOCK), BF16),
        V((NZ, NXY, 2 * CAP, BLOCK), BF16),
    ]
    dma = pltpu.SemaphoreType.DMA
    outs = (
        jax.ShapeDtypeStruct((OWN_BLOCKS, BLOCK, BLOCK), BF16),
        jax.ShapeDtypeStruct((ROOTS, 2 * BLOCK), BF16),
        jax.ShapeDtypeStruct((2 * BLOCK, BLOCK), F32),
        jax.ShapeDtypeStruct((2 * BLOCK, BLOCK), F32),
    )
    results = pl.pallas_call(
        main_kernel,
        out_shape=outs,
        in_specs=[vmem, vmem, vmem, hbm, hbm, hbm, vmem, vmem, vmem, vmem],
        out_specs=(hbm, hbm, vmem, vmem),
        scratch_shapes=[
            V((8, 256), jnp.int32),
            pltpu.SMEM((8, 256), jnp.int32),
            V((CAP, 2 * NZ * NXY), jnp.int32),
            pltpu.SMEM((CAP, 2 * NZ * NXY), jnp.int32),
            V((NZ, PLANE), jnp.int32),
            V((2 * BLOCK, 2 * BLOCK), BF16),
            V((OWN_BLOCKS, BLOCK, BLOCK), BF16),
            V((OWN_BLOCKS, BLOCK, BLOCK), BF16),
            V((ROOTS, 2 * BLOCK), BF16),
            V((ROOTS, 2 * BLOCK), BF16),
            V((TILES, BLOCK, BLOCK), BF16),
            V((OWN_BLOCKS, BLOCK, BLOCK), BF16),
            V((OWN_BLOCKS, BLOCK, BLOCK), F32),
            V((TILES + 1, BLOCK, BLOCK), F32),
            V((OWN_BLOCKS, BLOCK, BLOCK), F32),
            V((OWN_BLOCKS, BLOCK, BLOCK), F32),
            V((ROOTS + CAP, BLOCK), F32),
            V((OWN_BLOCKS, BLOCK, BLOCK), BF16),
            V((DEST_BLOCKS + 1, BLOCK, BLOCK), BF16),
            V((BLOCK, ROOTS), BF16),
            V((PLANE, BLOCK), F32),
            *exchange_bufs,
            *exchange_bufs,
            V((2, NXY, PART, BLOCK), F32),
            V((2, NXY, PART, BLOCK), F32),
            V((2, PART, BLOCK), F32),
            V((2, NZ, PART, BLOCK), F32),
            V((2, PART, BLOCK), F32),
            V((2, PART, BLOCK), F32),
            V((2, NXY, PART, BLOCK), F32),
            dma((LOADS + 4,)),
            dma((2, NZ)), dma((2, NZ)), dma((2, NZ)), dma((2, NZ)), dma((2, NZ)), dma((2, NZ)),
            dma((2,)),
            dma((2, 4)), dma((2, 4)), dma((2,)),
        ],
        compiler_params=pltpu.CompilerParams(has_side_effects=True, collective_id=1, vmem_limit_bytes=60 << 20),
        name="layer",
    )(
        tile_at.T, clone_root[0].T, clone_count, features, adjacency, cotangent.reshape(OWN_BLOCKS, BLOCK, BLOCK),
        bias_vector.reshape(1, BLOCK), degrees.reshape(OWN_BLOCKS, BLOCK), w_self, w_neigh,
    )
    act, gfeat, gself, gneigh = pl.pallas_call(
        finish_kernel,
        out_shape=outs,
        in_specs=[hbm] * 4,
        out_specs=(hbm,) * 4,
        scratch_shapes=[
            V((OWN_BLOCKS, BLOCK, BLOCK), BF16), V((ROOTS, 2 * BLOCK), BF16),
            V((2 * BLOCK, BLOCK), F32), V((2 * BLOCK, BLOCK), F32), dma((8,)), dma((8,)),
        ],
        compiler_params=pltpu.CompilerParams(vmem_limit_bytes=60 << 20),
        name="finish",
    )(*results)
    return act.reshape(ROOTS, BLOCK), gfeat, gself, gneigh


def solution(mesh):
    split = ("dom", "local")
    placed = (
        P(split, None), P(), P(), P(), P(split, None, None), P(split, None), P(split, None, None),
        P(split, None), P(split), P(split, None),
    )
    return jax.shard_map(
        per_device,
        mesh=mesh,
        in_specs=placed,
        out_specs=(P(split, None), P(split, None), P(), P()),
        check_vma=False,
    )
```

```python
import functools

import jax
import jax.numpy as jnp
from jax import lax
from jax.experimental import pallas as pl
from jax.experimental.pallas import tpu as pltpu
from jax.sharding import PartitionSpec as P

MESH = pl.DeviceIdType.MESH
F32 = jnp.float32
BF16 = jnp.bfloat16

NZ, NY, NX = 8, 4, 4
NXY = NY * NX
CAP = 8
BLOCK = 128
TILES = 192
OWN_BLOCKS = 32
CLONE_BLOCKS = 16
DEST_BLOCKS = OWN_BLOCKS + CLONE_BLOCKS
ROOTS = OWN_BLOCKS * BLOCK
MOST_OWN = TILES - CLONE_BLOCKS
MOST_CLONE = TILES - OWN_BLOCKS
PLANE = NXY * 2 * CAP
LOADS = 4

FWD, BWD, LAST_FWD, LAST_BWD = 0, 1, 2, 3
PART = 2 * BLOCK // NXY


def step_offset(i):
    return 4 + (i // 2) * (1 - i % 2) - ((i + 1) // 2) * (i % 2)


def make_table(tiles_at, out):
    across = lax.broadcasted_iota(jnp.int32, (TILES, TILES), 1)
    down = lax.broadcasted_iota(jnp.int32, (TILES, TILES), 0)

    def column(row):
        return jnp.sum(jnp.where(across == down, row, 0), axis=1, keepdims=True)

    dest = tiles_at[0:1, :]
    source = tiles_at[1:2, :]
    dest_c = column(dest)
    source_c = column(source)
    tile_c = lax.broadcasted_iota(jnp.int32, (TILES, 1), 0)
    tile = lax.broadcasted_iota(jnp.int32, (1, TILES), 1)
    is_clone = dest_c >= OWN_BLOCKS
    block = lax.broadcasted_iota(jnp.int32, (TILES, BLOCK), 1)
    key_b = source + jnp.where(dest >= OWN_BLOCKS, OWN_BLOCKS, 0)
    key_b_c = source_c + jnp.where(is_clone, OWN_BLOCKS, 0)
    code_f = tile_c + source_c * 256
    code_b = tile_c + jnp.where(is_clone, DEST_BLOCKS, dest_c) * 256 + jnp.where(is_clone, dest_c, DEST_BLOCKS) * 65536
    for at, last, key, key_c, code in ((FWD, LAST_FWD, dest, dest_c, code_f), (BWD, LAST_BWD, key_b, key_b_c, code_b)):
        before = (key * TILES + tile) < (key_c * TILES + tile_c)
        rank = jnp.sum(jnp.where(before, 1, 0), axis=1, keepdims=True)
        same = jnp.sum(jnp.where(before & (key == key_c), 1, 0), axis=1, keepdims=True)
        code = code + jnp.where(same > 0, 1 << 24, 0)
        out[at:at + 1, 0:TILES] = jnp.sum(jnp.where(rank == across, code, 0), axis=0, keepdims=True)
        upto = jnp.sum(jnp.where(key_c <= block, 1, 0), axis=0, keepdims=True) - 1
        if at == BWD:
            has = jnp.sum(jnp.where(key_c == block, 1, 0), axis=0, keepdims=True) > 0
            lane = lax.broadcasted_iota(jnp.int32, (1, BLOCK), 1)
            own = jnp.where(has, upto, TILES)
            clone = jnp.where(has, upto - OWN_BLOCKS, TILES)
            upto = jnp.where(lane < OWN_BLOCKS, own, clone)
        out[last:last + 1, 0:BLOCK] = upto


def main_kernel(
    tiles_at, root_t, count, features_h, adjacency_h, cotangent_h, bias, degrees, w_self, w_neigh,
    act_out, gfeat_out, gself_out, gneigh_out,
    table_v, table, slot_n, slot_s, slot_v, weights, cotangent, act, gfeat,
    feat, adj, proj, own, scan, total, scale, gmean, gpre, slots_t, gproj_t, rows_f,
    keep1, pass1, mate1, send1, mid1, land1,
    keep2, pass2, mate2, send2, mid2, land2,
    pieces, xy_r, sum_xy, z_r, sum_z, mate_r, done,
    load_sems, mate_send, mate_recv, xy_send, xy_recv, z_send, z_recv, own_sems,
    red_send, red_recv, out_sems,
):
    dom = lax.axis_index("dom")
    x = lax.axis_index("local")
    core = dom % 2
    zy = dom // 2
    z = zy // NY
    y = zy % NY
    xy = y * NX + x
    mate = (dom + 1 - 2 * core, x)

    def xy_peer(k):
        py = lax.rem(y + k // NX, NY)
        px = lax.rem(x + k % NX, NX)
        return (z * NY + py) * 2 + core, px, py * NX + px

    def z_peer(dz):
        pz = lax.rem(z + dz, NZ)
        return ((pz * NY + y) * 2 + core, x), pz

    barrier = pltpu.get_barrier_semaphore()
    pl.semaphore_signal(barrier, inc=1, device_id=mate, device_id_type=MESH)
    for k in range(1, NXY):
        pdom, px, _ = xy_peer(k)
        pl.semaphore_signal(barrier, inc=1, device_id=(pdom, px), device_id_type=MESH)
    for dz in range(1, NZ):
        pl.semaphore_signal(barrier, inc=1, device_id=z_peer(dz)[0], device_id_type=MESH)

    load_feat = pltpu.make_async_copy(features_h, feat, load_sems.at[LOADS])
    load_feat.start()
    share = TILES // LOADS
    load_adj = [
        pltpu.make_async_copy(
            adjacency_h.at[pl.ds(k * share, share)], adj.at[pl.ds(k * share, share)], load_sems.at[k]
        )
        for k in range(LOADS)
    ]
    for copy in load_adj:
        copy.start()
    load_cot = pltpu.make_async_copy(cotangent_h, cotangent, load_sems.at[LOADS + 1])
    load_cot.start()

    make_table(tiles_at[...], table_v)
    live = lax.broadcasted_iota(jnp.int32, (CAP, 2 * NZ * NXY), 0) < count[...]
    slot_n[...] = jnp.where(live, root_t[...], ROOTS)
    table_copy = pltpu.make_async_copy(table_v, table, load_sems.at[LOADS + 2])
    slot_copy = pltpu.make_async_copy(slot_n, slot_s, load_sems.at[LOADS + 3])
    table_copy.start()
    slot_copy.start()

    weights[:, 0:BLOCK] = w_neigh[...]
    weights[:, BLOCK:2 * BLOCK] = w_self[...]

    load_feat.wait()
    rows = 512

    def project(i, carry):
        both = jnp.dot(feat[pl.ds(i * rows, rows), :], weights[...], preferred_element_type=F32)
        proj[pl.ds(i * (rows // BLOCK), rows // BLOCK)] = both[:, :BLOCK].astype(BF16).reshape(rows // BLOCK, BLOCK, BLOCK)
        own[pl.ds(i * (rows // BLOCK), rows // BLOCK)] = (both[:, BLOCK:] + bias[...]).reshape(rows // BLOCK, BLOCK, BLOCK)
        return carry

    lax.fori_loop(0, ROOTS // rows, project, 0, unroll=4)
    for copy in load_adj:
        copy.wait()
    table_copy.wait()
    slot_copy.wait()

    def forward(i, acc):
        code = table[FWD, i]
        tile = code & 255
        source = (code >> 8) & 255
        going = (code >> 24).astype(F32)
        acc = acc * going + jnp.dot(adj[tile], proj[source], preferred_element_type=F32)
        scan[i] = acc
        return acc

    lax.fori_loop(0, TILES, forward, jnp.zeros((BLOCK, BLOCK), F32), unroll=48)

    pl.semaphore_wait(barrier, 1 + (NXY - 1) + (NZ - 1))

    def start_swap(i, value, keep, away, back, lane):
        first = value[:, 0]
        second = value[:, 1]
        keep[i] = jnp.where(core == 0, first, second).reshape(NXY * CAP, BLOCK).astype(BF16)
        away[i] = jnp.where(core == 0, second, first).reshape(NXY * CAP, BLOCK).astype(BF16)
        swap(i, away, back, lane).start()

    def swap(i, away, back, lane):
        return pltpu.make_async_remote_copy(
            away.at[i], back.at[i], mate_send.at[lane, i], mate_recv.at[lane, i], device_id=mate, device_id_type=MESH
        )

    def start_xy(i, keep, away, back, send, mid, lane):
        swap(i, away, back, lane).wait()
        mine = keep[i].astype(F32).reshape(NXY, CAP, BLOCK)
        theirs = back[i].astype(F32).reshape(NXY, CAP, BLOCK)
        first = jnp.where(core == 0, mine, theirs)
        second = jnp.where(core == 0, theirs, mine)
        send[i] = jnp.concatenate([first, second], axis=1).astype(BF16)

        for k in range(1, NXY):
            pdom, px, pxy = xy_peer(k)
            pltpu.make_async_remote_copy(
                send.at[i, pxy], mid.at[i, xy], xy_send.at[lane, i], xy_recv.at[lane, i],
                device_id=(pdom, px), device_id_type=MESH,
            ).start()
        mid[i, xy] = send[i, xy]

    def wait_bytes(ref, sem):
        pltpu.make_async_copy(ref, ref, sem).wait()

    def z_copy(i, mid, land, lane):
        peer, _ = z_peer(step_offset(i))
        return pltpu.make_async_remote_copy(
            mid.at[i], land.at[z], z_send.at[lane, i], z_recv.at[lane, i], device_id=peer, device_id_type=MESH
        )

    def start_z(i, send, mid, land, lane):
        wait_bytes(mid.at[i, pl.ds(0, NXY - 1)], xy_recv.at[lane, i])
        wait_bytes(send.at[i, pl.ds(0, NXY - 1)], xy_send.at[lane, i])

        if isinstance(i, int) and i < NZ - 1:
            z_copy(i, mid, land, lane).start()
        elif isinstance(i, int):
            pltpu.make_async_copy(mid.at[i], land.at[z], own_sems.at[lane]).start()
        else:
            @pl.when(i < NZ - 1)
            def _():
                z_copy(i, mid, land, lane).start()

            @pl.when(i == NZ - 1)
            def _():
                pltpu.make_async_copy(mid.at[i], land.at[z], own_sems.at[lane]).start()

    def finish_z(i, mid, land, lane):
        @pl.when(i < NZ - 1)
        def _():
            z_copy(i, mid, land, lane).wait()

        @pl.when(i == NZ - 1)
        def _():
            pltpu.make_async_copy(mid.at[i], land.at[z], own_sems.at[lane]).wait()

        return (z + NZ - step_offset(i)) % NZ

    def send_partial(s, carry):
        pz = (z + step_offset(s)) % NZ
        first = scan[table[LAST_FWD, OWN_BLOCKS + 2 * pz]]
        second = scan[table[LAST_FWD, OWN_BLOCKS + 2 * pz + 1]]
        value = jnp.concatenate([first, second], axis=0).reshape(NY, 2, NX, CAP, BLOCK)
        value = jnp.concatenate([value[:, 0].reshape(NXY, 1, CAP, BLOCK), value[:, 1].reshape(NXY, 1, CAP, BLOCK)], axis=1)
        start_swap(s, value, keep1, pass1, mate1, 0)
        return carry

    lax.fori_loop(0, NZ, send_partial, 0)

    def send_xy(s, carry):
        start_xy(s, keep1, pass1, mate1, send1, mid1, 0)
        return carry

    lax.fori_loop(0, NZ, send_xy, 0)

    def send_z(s, carry):
        start_z(s, send1, mid1, land1, 0)
        return carry

    lax.fori_loop(0, NZ, send_z, 0)

    node = slot_n[...].astype(F32)
    high = jnp.floor(node * (1.0 / 64.0))
    low = node - high * 64.0
    both = jnp.concatenate([high, low], axis=0).astype(BF16)
    lane = lax.broadcasted_iota(jnp.int32, (2 * NZ * NXY, PLANE), 1)
    device = (lane // 64) * 8 + ((lane // 8) % 2) * 4 + (lane // 16) % 4
    down = lax.broadcasted_iota(jnp.int32, (2 * NZ * NXY, PLANE), 0)
    lane_cap = lax.broadcasted_iota(jnp.int32, (CAP, PLANE), 1) % CAP
    down_cap = lax.broadcasted_iota(jnp.int32, (CAP, PLANE), 0)
    for p in range(NZ):
        pick = jnp.where(down == device + p * 2 * NXY, 1.0, 0.0).astype(BF16)
        value = jnp.dot(both, pick, preferred_element_type=F32)
        value = value[0:CAP] * 64.0 + value[CAP:2 * CAP]
        slot_v[p:p + 1, :] = jnp.sum(jnp.where(lane_cap == down_cap, value, 0.0), axis=0, keepdims=True).astype(jnp.int32)
    def begin_total(b, carry):
        total[b] = scan[table[LAST_FWD, b]]
        inverse = 1.0 / degrees[pl.ds(b, 1), :].astype(F32)
        scale[b] = jnp.broadcast_to(inverse, (BLOCK, BLOCK)).T
        return carry

    lax.fori_loop(0, OWN_BLOCKS, begin_total, 0, unroll=2)

    def receive_plane(s, carry):
        plane = finish_z((s + NZ - 1) % NZ, mid1, land1, 0)
        arrived = land1[plane].reshape(PLANE, BLOCK)
        node = slot_v[pl.ds(plane, 1), :]
        row = lax.broadcasted_iota(jnp.int32, (BLOCK, PLANE), 0)

        def add(b, carry):
            hit = jnp.where(row == node - b * BLOCK, 1.0, 0.0).astype(BF16)
            total[b] += jnp.dot(hit, arrived, preferred_element_type=F32)
            return carry

        lax.fori_loop(0, OWN_BLOCKS, add, 0, unroll=OWN_BLOCKS)
        return carry

    lax.fori_loop(0, NZ, receive_plane, 0)
    load_cot.wait()

    def activate(b, carry):
        preact = own[b] + total[b] * scale[b]
        sig = jax.nn.sigmoid(preact)
        act[b] = (preact * sig).astype(BF16)
        full = cotangent[b].astype(F32) * sig * (1.0 + preact * (1.0 - sig))
        gpre[b] = full.astype(BF16)
        gmean[pl.ds(b * BLOCK, BLOCK), :] = full * scale[b]
        return carry

    lax.fori_loop(0, OWN_BLOCKS, activate, 0, unroll=4)
    give_act = pltpu.make_async_copy(act, act_out, out_sems.at[0])
    give_act.start()
    gmean[pl.ds(ROOTS, CAP), :] = jnp.zeros((CAP, BLOCK), F32)
    slots_t[DEST_BLOCKS] = jnp.zeros((BLOCK, BLOCK), BF16)
    scan[TILES] = jnp.zeros((BLOCK, BLOCK), F32)

    def back_own(i, acc):
        code = table[BWD, i]
        tile = code & 255
        dest = (code >> 8) & 255
        going = (code >> 24).astype(F32)
        acc = acc * going + jnp.dot(slots_t[dest], adj[tile], preferred_element_type=F32)
        scan[i] = acc
        return acc

    def gather_plane(s, carry):
        pz = (z + step_offset(s)) % NZ

        for q in range(2 * NXY):
            d = pz * 2 * NXY + (q // 8) * 8 + (q % 2) * 4 + (q // 2) % 4
            for j in range(CAP):
                rows_f[q * CAP + j:q * CAP + j + 1, :] = gmean[pl.ds(slot_s[j, d], 1), :]
        start_swap(s, rows_f[...].reshape(NXY, 2, CAP, BLOCK), keep2, pass2, mate2, 1)
        return carry

    def send_back(s, carry):
        gather_plane(s, 0)

        @pl.when(s >= 3)
        def _():
            start_xy(s - 3, keep2, pass2, mate2, send2, mid2, 1)

        return carry

    lax.fori_loop(0, NZ, send_back, 0)
    def transpose(b, carry):
        at = pl.ds(pl.multiple_of(b * BLOCK, BLOCK), BLOCK)
        gproj_t[:, at] = gpre[b].astype(F32).T.astype(BF16)
        slots_t[b] = gmean[pl.ds(b * BLOCK, BLOCK), :].T.astype(BF16)
        return carry

    for k in range(3):
        start_xy(NZ - 3 + k, keep2, pass2, mate2, send2, mid2, 1)
        start_z(k, send2, mid2, land2, 1)
    lax.fori_loop(0, OWN_BLOCKS // 2, transpose, 0, unroll=4)
    start_z(3, send2, mid2, land2, 1)
    start_z(4, send2, mid2, land2, 1)
    lax.fori_loop(OWN_BLOCKS // 2, OWN_BLOCKS, transpose, 0, unroll=4)
    start_z(5, send2, mid2, land2, 1)
    start_z(6, send2, mid2, land2, 1)
    start_z(7, send2, mid2, land2, 1)
    gself = jnp.dot(gproj_t[...], feat[...], preferred_element_type=F32).T

    def wait_both(ref, lane, k):
        wait_bytes(ref, red_recv.at[lane, k])
        wait_bytes(ref, red_send.at[lane, k])

    def around_xy(src, dst, lane, k):
        for j in range(1, NXY):
            pdom, px, pxy = xy_peer(j)
            pltpu.make_async_remote_copy(
                src(pxy), dst, red_send.at[lane, k], red_recv.at[lane, k],
                device_id=(pdom, px), device_id_type=MESH,
            ).start()

    def swap_sums(lane):
        return pltpu.make_async_remote_copy(
            sum_z.at[lane], mate_r.at[lane], red_send.at[lane, 2], red_recv.at[lane, 2],
            device_id=mate, device_id_type=MESH,
        )

    def reduce_0(value, lane):
        pieces[lane] = value.reshape(NXY, PART, BLOCK)
        around_xy(lambda pxy: pieces.at[lane, pxy], xy_r.at[lane, xy], lane, 0)
        xy_r[lane, xy] = pieces[lane, xy]

    def reduce_1(lane):
        wait_both(xy_r.at[lane, pl.ds(0, NXY - 1)], lane, 0)
        value = xy_r[lane, 0]
        for k in range(1, NXY):
            value = value + xy_r[lane, k]
        sum_xy[lane] = value

        for dz in range(1, NZ):
            peer, _ = z_peer(dz)
            pltpu.make_async_remote_copy(
                sum_xy.at[lane], z_r.at[lane, z], red_send.at[lane, 1], red_recv.at[lane, 1],
                device_id=peer, device_id_type=MESH,
            ).start()
        z_r[lane, z] = value

    def reduce_2(lane):
        wait_both(z_r.at[lane, pl.ds(0, NZ - 1)], lane, 1)
        value = z_r[lane, 0]
        for k in range(1, NZ):
            value = value + z_r[lane, k]
        sum_z[lane] = value
        swap_sums(lane).start()

    def reduce_3(lane):
        swap_sums(lane).wait()
        done[lane, xy] = (sum_z[lane] + mate_r[lane]) * (float(ROOTS * 2 * NZ * NXY) ** -0.5)
        around_xy(lambda pxy: done.at[lane, xy], done.at[lane, xy], lane, 3)

    def reduce_4(lane, out):
        wait_both(done.at[lane, pl.ds(0, NXY - 1)], lane, 3)
        out[...] = done[lane].reshape(2 * BLOCK, BLOCK)

    reduce_0(gself, 0)
    lax.fori_loop(0, MOST_OWN, back_own, jnp.zeros((BLOCK, BLOCK), F32), unroll=22)

    def keep_own(c, carry):
        total[c] = scan[table[LAST_BWD, c]]
        return carry

    lax.fori_loop(0, OWN_BLOCKS, keep_own, 0, unroll=4)

    def arrived_back(s, carry):
        plane = finish_z((s + NZ - 1) % NZ, mid2, land2, 1)
        value = land2[plane].astype(F32).reshape(NY, NX, 2, CAP, BLOCK)
        value = jnp.concatenate(
            [value[:, :, 0].reshape(NY, 1, NX, CAP, BLOCK), value[:, :, 1].reshape(NY, 1, NX, CAP, BLOCK)], axis=1
        ).reshape(2, BLOCK, BLOCK)
        slots_t[OWN_BLOCKS + 2 * plane] = value[0].T.astype(BF16)
        slots_t[OWN_BLOCKS + 2 * plane + 1] = value[1].T.astype(BF16)
        return carry

    lax.fori_loop(0, NZ, arrived_back, 0)
    reduce_1(0)

    def back_clone(i, acc):
        code = table[BWD, OWN_BLOCKS + i]
        tile = code & 255
        dest = (code >> 16) & 255
        going = (code >> 24).astype(F32)
        acc = acc * going + jnp.dot(slots_t[dest], adj[tile], preferred_element_type=F32)
        scan[i] = acc
        return acc

    lax.fori_loop(0, MOST_CLONE, back_clone, jnp.zeros((BLOCK, BLOCK), F32), unroll=40)

    def gather_proj(c, carry):
        value = total[c] + scan[table[LAST_BWD, OWN_BLOCKS + c]]
        at = pl.ds(pl.multiple_of(c * BLOCK, BLOCK), BLOCK)
        gproj_t[:, at] = value.astype(BF16)
        return carry

    lax.fori_loop(0, OWN_BLOCKS, gather_proj, 0, unroll=16)
    reduce_2(0)
    gneigh = jnp.dot(gproj_t[...], feat[...], preferred_element_type=F32).T

    reduce_0(gneigh, 1)
    reduce_3(0)

    def give_features(c, carry):
        at = pl.ds(pl.multiple_of(c * BLOCK, BLOCK), BLOCK)
        value = lax.dot_general(gpre[c], w_self[...], (((1,), (1,)), ((), ())), preferred_element_type=F32)
        value += lax.dot_general(gproj_t[:, at], w_neigh[...], (((0,), (1,)), ((), ())), preferred_element_type=F32)
        gfeat[pl.ds(c * BLOCK, BLOCK), :] = value.astype(BF16)
        return carry

    lax.fori_loop(0, OWN_BLOCKS // 4, give_features, 0, unroll=8)
    reduce_1(1)
    lax.fori_loop(OWN_BLOCKS // 4, OWN_BLOCKS // 2, give_features, 0, unroll=8)
    reduce_2(1)
    lax.fori_loop(OWN_BLOCKS // 2, OWN_BLOCKS // 4 * 3, give_features, 0, unroll=8)
    reduce_3(1)
    lax.fori_loop(OWN_BLOCKS // 4 * 3, OWN_BLOCKS, give_features, 0, unroll=8)
    give_feat = pltpu.make_async_copy(gfeat, gfeat_out, out_sems.at[1])
    give_feat.start()
    reduce_4(0, gself_out)
    reduce_4(1, gneigh_out)
    give_act.wait()
    give_feat.wait()


def finish_kernel(act, gfeat, gself, gneigh, act_out, gfeat_out, gself_out, gneigh_out, act_v, gfeat_v, gself_v, gneigh_v, load, give):
    copies = []
    for src, mid, dst, cuts in (
        (gfeat, gfeat_v, gfeat_out, 4), (act, act_v, act_out, 2), (gself, gself_v, gself_out, 1), (gneigh, gneigh_v, gneigh_out, 1)
    ):
        rows = src.shape[0] // cuts
        for k in range(cuts):
            at = pl.ds(k * rows, rows)
            n = len(copies)
            copies.append((
                pltpu.make_async_copy(src.at[at], mid.at[at], load.at[n]),
                pltpu.make_async_copy(mid.at[at], dst.at[at], give.at[n]),
            ))
    for into, _ in copies:
        into.start()
    for into, out in copies:
        into.wait()
        out.start()
    for _, out in copies:
        out.wait()


def per_device(
    features, w_self, w_neigh, bias_vector, adjacency, tile_at, clone_root, clone_count, degrees, cotangent
):
    vmem = pl.BlockSpec(memory_space=pltpu.VMEM)
    hbm = pl.BlockSpec(memory_space=pl.ANY)
    V = pltpu.VMEM
    exchange_bufs = [
        V((NZ, NXY * CAP, BLOCK), BF16),
        V((NZ, NXY * CAP, BLOCK), BF16),
        V((NZ, NXY * CAP, BLOCK), BF16),
        V((NZ, NXY, 2 * CAP, BLOCK), BF16),
        V((NZ, NXY, 2 * CAP, BLOCK), BF16),
        V((NZ, NXY, 2 * CAP, BLOCK), BF16),
    ]
    dma = pltpu.SemaphoreType.DMA
    outs = (
        jax.ShapeDtypeStruct((OWN_BLOCKS, BLOCK, BLOCK), BF16),
        jax.ShapeDtypeStruct((ROOTS, 2 * BLOCK), BF16),
        jax.ShapeDtypeStruct((2 * BLOCK, BLOCK), F32),
        jax.ShapeDtypeStruct((2 * BLOCK, BLOCK), F32),
    )
    results = pl.pallas_call(
        main_kernel,
        out_shape=outs,
        in_specs=[vmem, vmem, vmem, hbm, hbm, hbm, vmem, vmem, vmem, vmem],
        out_specs=(hbm, hbm, vmem, vmem),
        scratch_shapes=[
            V((8, 256), jnp.int32),
            pltpu.SMEM((8, 256), jnp.int32),
            V((CAP, 2 * NZ * NXY), jnp.int32),
            pltpu.SMEM((CAP, 2 * NZ * NXY), jnp.int32),
            V((NZ, PLANE), jnp.int32),
            V((2 * BLOCK, 2 * BLOCK), BF16),
            V((OWN_BLOCKS, BLOCK, BLOCK), BF16),
            V((OWN_BLOCKS, BLOCK, BLOCK), BF16),
            V((ROOTS, 2 * BLOCK), BF16),
            V((ROOTS, 2 * BLOCK), BF16),
            V((TILES, BLOCK, BLOCK), BF16),
            V((OWN_BLOCKS, BLOCK, BLOCK), BF16),
            V((OWN_BLOCKS, BLOCK, BLOCK), F32),
            V((TILES + 1, BLOCK, BLOCK), F32),
            V((OWN_BLOCKS, BLOCK, BLOCK), F32),
            V((OWN_BLOCKS, BLOCK, BLOCK), F32),
            V((ROOTS + CAP, BLOCK), F32),
            V((OWN_BLOCKS, BLOCK, BLOCK), BF16),
            V((DEST_BLOCKS + 1, BLOCK, BLOCK), BF16),
            V((BLOCK, ROOTS), BF16),
            V((PLANE, BLOCK), F32),
            *exchange_bufs,
            *exchange_bufs,
            V((2, NXY, PART, BLOCK), F32),
            V((2, NXY, PART, BLOCK), F32),
            V((2, PART, BLOCK), F32),
            V((2, NZ, PART, BLOCK), F32),
            V((2, PART, BLOCK), F32),
            V((2, PART, BLOCK), F32),
            V((2, NXY, PART, BLOCK), F32),
            dma((LOADS + 4,)),
            dma((2, NZ)), dma((2, NZ)), dma((2, NZ)), dma((2, NZ)), dma((2, NZ)), dma((2, NZ)),
            dma((2,)),
            dma((2, 4)), dma((2, 4)), dma((2,)),
        ],
        compiler_params=pltpu.CompilerParams(has_side_effects=True, collective_id=1, vmem_limit_bytes=60 << 20),
        name="layer",
    )(
        tile_at.T, clone_root[0].T, clone_count, features, adjacency, cotangent.reshape(OWN_BLOCKS, BLOCK, BLOCK),
        bias_vector.reshape(1, BLOCK), degrees.reshape(OWN_BLOCKS, BLOCK), w_self, w_neigh,
    )
    act, gfeat, gself, gneigh = pl.pallas_call(
        finish_kernel,
        out_shape=outs,
        in_specs=[hbm] * 4,
        out_specs=(hbm,) * 4,
        scratch_shapes=[
            V((OWN_BLOCKS, BLOCK, BLOCK), BF16), V((ROOTS, 2 * BLOCK), BF16),
            V((2 * BLOCK, BLOCK), F32), V((2 * BLOCK, BLOCK), F32), dma((8,)), dma((8,)),
        ],
        compiler_params=pltpu.CompilerParams(vmem_limit_bytes=60 << 20),
        name="finish",
    )(*results)
    return act.reshape(ROOTS, BLOCK), gfeat, gself, gneigh


def solution(mesh):
    split = ("dom", "local")
    placed = (
        P(split, None), P(), P(), P(), P(split, None, None), P(split, None), P(split, None, None),
        P(split, None), P(split), P(split, None),
    )
    return jax.shard_map(
        per_device,
        mesh=mesh,
        in_specs=placed,
        out_specs=(P(split, None), P(split, None), P(), P()),
        check_vma=False,
    )
```
